512 devices in a mesh: seq: 128 (over z, x, core), dp: 4 (over y).
Axes of the slice: x: 4, y: 4, z: 16, core: 2. Of those that a mesh axis runs over, the one named last changes fastest.
Arguments:
- queries: bfloat16 [4, 32768, 512], P('dp', 'seq'), may hold values from -1.75 to 1.75
- keys: bfloat16 [4, 32768, 512], P('dp', 'seq'), may hold values from -1.75 to 1.75
- values: bfloat16 [4, 32768, 512], P('dp', 'seq'), may hold values from -6 to 6
- gates: bfloat16 [4, 32768, 512], P('dp', 'seq'), may hold values from -24 to 24
- out_weight: bfloat16 [512, 1024], replicated, may hold values from -0.25 to 0.25
- out_grad: bfloat16 [4, 32768, 1024], P('dp', 'seq'), may hold values from -6 to 6
- lengths: int32 [4, 4], P('dp'), may hold values from 1 to 16384, 32768 in all within a row
- pattern: int32 [4, 128, 2], P('dp', 'seq'), may hold values 0 or 1
Outputs:
- query_grad: bfloat16 [4, 32768, 512], P('dp', 'seq')
- key_grad: bfloat16 [4, 32768, 512], P('dp', 'seq')
- value_grad: bfloat16 [4, 32768, 512], P('dp', 'seq')
- gate_grad: bfloat16 [4, 32768, 512], P('dp', 'seq')
- weight_grad: float32 [512, 1024], P('seq')
The draws below stay inside these ranges and needn't reach their ends.
Inputs may be any that keep to these rules, and one draw needn't show every extreme that they name: Each row of lengths sums to 32768, and its largest entry is exactly 16384.
All inputs are finite; a program needn't handle non-finite values. No bound on the sum of `pattern` on one device may be relied on, other than what follows from the above.
Results may differ from the reference program's by a relative error of at most 0.0065.
Values may be sent and summed in bfloat16 or wider, within the bound.
A program may use at most 64 MiB of HBM per device.

```python
import math
import jax
import jax.numpy as jnp
import numpy as np
from jax import lax

D = 1024
HEADS = 4
HEAD_DIM = 128
ROWS_DEV = 256
BAND = 2
SEQS = 4
HD = 512
TOK_SEQ = 32768
N_SEQ = 128
N_DP = 4


def touch_ends(entries, key, smallest, largest):
    longest = entries.shape.index(max(entries.shape))
    spots = []
    for shift in (0, 1):
        where = [jax.random.randint(jax.random.fold_in(key, axis), (), 0, length) for axis, length in enumerate(entries.shape)]
        where[longest] = (where[longest] + shift) % entries.shape[longest]
        spots.append(tuple(where))
    return entries.at[spots[0]].set(smallest).at[spots[1]].set(largest)


def raised(result, key, source, target, shards_of, factor):
    def block_of(axis_at):
        return (jnp.arange(result.shape[axis_at]) // (result.shape[axis_at] // shards_of)).reshape((-1,) + (1,) * (result.ndim - 1 - axis_at))

    near = jax.random.permutation(key, shards_of)[block_of(target)]
    second = (block_of(target) + shards_of // 2) % shards_of
    return jnp.where((block_of(source) == near) | (block_of(source) == second), factor * result, result)


def steps_of(rng, extent, shards, least, largest):
    def one(position, parts):
        heights = jax.random.uniform(jax.random.fold_in(jax.random.fold_in(rng, 6), position), (parts,), jnp.float32, least / len(shards), largest / len(shards))
        return jnp.repeat(jnp.exp(heights), extent[position] // parts).reshape((-1,) + (1,) * (len(extent) - position - 1))

    loudness = one(*shards[0])
    for cut in shards[1:]:
        loudness = loudness * one(*cut)
    return loudness


def profile(amount, total, reach, slope):
    portions = [(1 << 20) // math.isqrt(standing ** slope) + 1 for standing in range(2, amount + 1)]
    spare, counts = total - reach - (amount - 1), [1] * (amount - 1)
    while spare > 0:
        free = [i for i in range(amount - 1) if counts[i] < reach]
        mass, left = sum([portions[i] for i in free]), spare
        for i in free:
            addition = min(reach - counts[i], max(1, left * portions[i] // mass), spare)
            counts[i] = counts[i] + addition
            spare = spare - addition
    return np.array([reach] + counts)


def uneven(key, amount, total, reach, slope):
    if amount == 2:
        one = jax.random.randint(key, (), max(1, total - reach), min(reach, total - 1) + 1)
        return jnp.stack([one, total - one])
    sizes = jnp.asarray(profile(amount, total, reach, slope), jnp.int32)
    twos = (amount - 1) // 2
    donor, sink = sizes[1:1 + 2 * twos:2], sizes[2:2 + 2 * twos:2]
    room = jnp.minimum(donor - 1, reach - sink)
    moved = jax.random.randint(jax.random.fold_in(key, 1), (twos,), 0, 1 << 20) % (room + 1)
    sizes = sizes.at[1:1 + 2 * twos:2].set(donor - moved).at[2:2 + 2 * twos:2].set(sink + moved)
    return sizes[jax.random.permutation(jax.random.fold_in(key, 2), amount)]


def noise(own_key, dims, deviation, bound, pieces=(), kind=jnp.bfloat16):
    values = jax.random.normal(own_key, dims, jnp.float32) * deviation
    if len(pieces) > 0:
        values = steps_of(own_key, dims, pieces, -0.22, 0.18) * values
    return jnp.clip(values, min=-bound, max=bound).astype(kind)


def gaussian_with(key, shape, deviation, most, pieces, heavy, held_as=jnp.bfloat16):
    drawn = deviation * jax.random.normal(key, shape, jnp.float32)
    if pieces:
        drawn = drawn * steps_of(key, shape, pieces, -0.22, 0.18)
    return jnp.clip(raised(drawn, jax.random.fold_in(key, 3), *heavy), -most, most).astype(held_as)


def setup_inputs(seed: int = 0) -> dict:
    splits = jax.random.split(jax.random.key(seed), 9)
    return {
        "queries": noise(splits[0], (N_DP, TOK_SEQ, HD), 0.3, 1.75, ((0, 4), (1, 128))),
        "keys": noise(splits[1], (N_DP, TOK_SEQ, HD), 0.3, 1.75, ((0, 4), (1, 128))),
        "values": noise(splits[2], (N_DP, TOK_SEQ, HD), 1.0, 6.0, ((0, 4), (1, 128))),
        "gates": gaussian_with(splits[3], (N_DP, TOK_SEQ, HD), 1.0, 24.0, ((0, 4), (1, 128)), (1, 2, 128, 5.5)),
        "out_weight": noise(splits[4], (HD, D), HD ** -0.5, 0.25),
        "out_grad": noise(splits[5], (N_DP, TOK_SEQ, D), 1.0, 6.0, ((0, 4), (1, 128))),
        "lengths": jax.vmap(lambda own: uneven(own, SEQS, TOK_SEQ, TOK_SEQ // 2, 2))(jax.random.split(splits[6], N_DP)).reshape((N_DP, SEQS)).astype(jnp.int32),
        "pattern": touch_ends((jax.random.randint(splits[7], (N_DP, N_SEQ, BAND), 0, 4) < 3).astype(jnp.int32), jax.random.fold_in(splits[7], 1), 0, 1),
    }


EPS = 1e-05

def silu_slope(scores):
    sigma = jax.nn.sigmoid(scores)
    return sigma * (1.0 + scores * (1.0 - sigma))

def visible(query_block, pattern_row, doc_ends, block_rows):
    offsets = jnp.arange(block_rows, dtype=jnp.int32)
    query_pos = query_block * block_rows + offsets
    key_block = query_block - jnp.arange(pattern_row.shape[0] + 1, dtype=jnp.int32)
    key_pos = (key_block[:, None] * block_rows + offsets[None, :]).reshape(-1)
    allowed = jnp.concatenate([jnp.ones((1,), jnp.float32), (pattern_row > 0).astype(jnp.float32)])
    allowed_keys = jnp.repeat(allowed, block_rows)
    query_doc = lax.optimization_barrier(jnp.sum((query_pos[:, None] >= doc_ends[None, :]).astype(jnp.int32), axis=1))
    key_doc = lax.optimization_barrier(jnp.sum((key_pos[:, None] >= doc_ends[None, :]).astype(jnp.int32), axis=1))
    keep = (query_doc[:, None] == key_doc[None, :]) & (key_pos[None, :] <= query_pos[:, None]) & (key_pos[None, :] >= 0)
    return keep.astype(jnp.float32) * allowed_keys[None, :]

def rounded(term):
    return lax.optimization_barrier(term.astype(jnp.bfloat16)).astype(jnp.float32)

def reference(queries, keys, values, gates, out_weight, out_grad, lengths, pattern):
    width = HEADS * HEAD_DIM
    nblock = queries.shape[1] // ROWS_DEV
    scale = 1.0 / ((BAND + 1) * ROWS_DEV)

    def blocks(array):
        return array.reshape(N_DP, nblock, ROWS_DEV, array.shape[-1])
    query_blocks = blocks(queries)
    key_blocks = blocks(keys)
    value_blocks = blocks(values)
    gate_blocks = blocks(gates)
    grad_blocks = blocks(out_grad)
    empty = jnp.zeros((N_DP, BAND, ROWS_DEV, width), jnp.bfloat16)
    key_padded = jnp.concatenate([empty, key_blocks], axis=1)
    value_padded = jnp.concatenate([empty, value_blocks], axis=1)
    doc_ends = jnp.cumsum(lengths, axis=1)

    def window(store, group, block):
        piece = lax.dynamic_slice(store, (group, block, jnp.int32(0), jnp.int32(0)), (1, BAND + 1, ROWS_DEV, width))[0]
        return piece[::-1].reshape((BAND + 1) * ROWS_DEV, HEADS, HEAD_DIM).astype(jnp.float32)

    def front(index):
        group = (index // nblock).astype(jnp.int32)
        block = (index % nblock).astype(jnp.int32)
        query_heads = query_blocks[group, block].reshape(ROWS_DEV, HEADS, HEAD_DIM).astype(jnp.float32)
        key_band = window(key_padded, group, block)
        value_band = window(value_padded, group, block)
        gate_rows = gate_blocks[group, block].astype(jnp.float32)
        grad_rows = grad_blocks[group, block]
        visible_mask = visible(block, pattern[group, block], doc_ends[group], ROWS_DEV)
        scores = jnp.einsum('qhd,khd->hqk', query_heads, key_band)
        weights = (jax.nn.silu(scores) * visible_mask[None] * scale).astype(jnp.bfloat16)
        mixed = jnp.einsum('hqk,khd->qhd', weights.astype(jnp.float32), value_band).reshape(ROWS_DEV, width)
        centre = lax.optimization_barrier(jnp.mean(mixed, axis=1, keepdims=True))
        spread = lax.optimization_barrier(jnp.mean((mixed - centre) ** 2, axis=1, keepdims=True))
        inv_root = lax.rsqrt(spread + EPS)
        normed = (mixed - centre) * inv_root
        gated = (normed * gate_rows).astype(jnp.bfloat16)
        gated_grad = jnp.dot(grad_rows, out_weight.T, preferred_element_type=jnp.float32)
        gate_grad = (gated_grad * normed).astype(jnp.bfloat16)
        normed_grad = gated_grad * gate_rows
        mixed_grad = inv_root * (normed_grad - lax.optimization_barrier(jnp.mean(normed_grad, axis=1, keepdims=True)) - normed * lax.optimization_barrier(jnp.mean(normed_grad * normed, axis=1, keepdims=True)))
        mixed_grad = mixed_grad.astype(jnp.bfloat16)
        grad_heads = mixed_grad.reshape(ROWS_DEV, HEADS, HEAD_DIM).astype(jnp.float32)
        weight_slope = jnp.einsum('qhd,khd->hqk', grad_heads, value_band)
        score_grad = (weight_slope * visible_mask[None] * scale * silu_slope(scores)).astype(jnp.bfloat16)
        query_grad = jnp.einsum('hqk,khd->qhd', score_grad.astype(jnp.float32), key_band)
        return (query_grad.reshape(ROWS_DEV, width).astype(jnp.bfloat16), gate_grad, mixed_grad, gated)
    query_grad, gate_grad, mixed_grad, gated = lax.map(front, jnp.arange(N_DP * nblock, dtype=jnp.int32))
    tail = jnp.zeros((N_DP, BAND, ROWS_DEV, width), jnp.bfloat16)
    query_padded = jnp.concatenate([query_blocks, tail], axis=1)
    mixed_padded = jnp.concatenate([mixed_grad.reshape(N_DP, nblock, ROWS_DEV, width), tail], axis=1)
    pattern_padded = jnp.concatenate([pattern, jnp.zeros((N_DP, BAND, BAND), jnp.int32)], axis=1)

    def back(index):
        group = (index // nblock).astype(jnp.int32)
        block = (index % nblock).astype(jnp.int32)
        key_heads = key_blocks[group, block].reshape(ROWS_DEV, HEADS, HEAD_DIM).astype(jnp.float32)
        value_heads = value_blocks[group, block].reshape(ROWS_DEV, HEADS, HEAD_DIM).astype(jnp.float32)
        key_total = jnp.zeros((ROWS_DEV, HEADS, HEAD_DIM), jnp.float32)
        value_total = jnp.zeros((ROWS_DEV, HEADS, HEAD_DIM), jnp.float32)
        for offset in range(BAND + 1):
            reader = block + offset
            far_heads = query_padded[group, reader].reshape(ROWS_DEV, HEADS, HEAD_DIM).astype(jnp.float32)
            far_grad = mixed_padded[group, reader].reshape(ROWS_DEV, HEADS, HEAD_DIM).astype(jnp.float32)
            far_mask = visible(reader, pattern_padded[group, reader], doc_ends[group], ROWS_DEV)
            far_mask = far_mask[:, offset * ROWS_DEV:(offset + 1) * ROWS_DEV]
            scores = jnp.einsum('qhd,khd->hqk', far_heads, key_heads)
            weights = (jax.nn.silu(scores) * far_mask[None] * scale).astype(jnp.bfloat16)
            weight_slope = jnp.einsum('qhd,khd->hqk', far_grad, value_heads)
            score_grad = (weight_slope * far_mask[None] * scale * silu_slope(scores)).astype(jnp.bfloat16)
            key_total = key_total + rounded(jnp.einsum('hqk,qhd->khd', score_grad.astype(jnp.float32), far_heads))
            value_total = value_total + rounded(jnp.einsum('hqk,qhd->khd', weights.astype(jnp.float32), far_grad))
        return (key_total.reshape(ROWS_DEV, width).astype(jnp.bfloat16), value_total.reshape(ROWS_DEV, width).astype(jnp.bfloat16))
    key_grad, value_grad = lax.map(back, jnp.arange(N_DP * nblock, dtype=jnp.int32))
    weight_grad = jnp.dot(gated.reshape(-1, width).T, out_grad.reshape(-1, D), preferred_element_type=jnp.float32)
    shape = (N_DP, nblock * ROWS_DEV, width)
    return (query_grad.reshape(shape), key_grad.reshape(shape), value_grad.reshape(shape), gate_grad.reshape(shape), weight_grad)
```

```python
import jax
import jax.numpy as jnp
from jax import lax
from jax.experimental import pallas as pl
from jax.experimental.pallas import tpu as pltpu
from jax.sharding import PartitionSpec as P

MESH = pl.DeviceIdType.MESH
EPS = 1e-05
HEADS = 4
HEAD_DIM = 128
ROWS = 256
WIDTH = 512
MODEL = 1024
NX = 4
NZ = 16
NY = 4
N_SEQ = 128
BAND = 2
PARTS = 2
PART = ROWS // PARTS
SCALE = 1.0 / ((BAND + 1) * ROWS)
BF16 = jnp.bfloat16
F32 = jnp.float32
NT = (((1,), (1,)), ((), ()))
TN = (((0,), (0,)), ((), ()))


def dot(a, b):
    return jnp.dot(a, b, preferred_element_type=F32)


def dot_nt(a, b):
    return lax.dot_general(a, b, NT, preferred_element_type=F32)


def dot_tn(a, b):
    return lax.dot_general(a, b, TN, preferred_element_type=F32)


def loop(n, body):
    lax.fori_loop(0, n, lambda i, c: (body(i), c)[1], jnp.int32(0))


def kernel(
    len_in, pat_in, q_in, k_in, v_in, gate_in, w_in, og_in,
    dq_out, dk_out, dv_out, dg_out, wg_out,
    len_ref, pat_ref, q3, kb, vb, gb, ogb, wb, mask, half, dgt, mix,
    ps, mr, d3, dsend, es, er, attn, slope, gt,
    gown, gs, gr, ya, yar, yb, ybr, xs, xr, zs, zr, tiles,
    dqa, dka, dva, dqo, dko, dvo, dgo,
    ld_sem, few_sem, out_sem, q_ss, q_rs, m_ss, m_rs, d_ss, d_rs, e_ss, e_rs,
    p_ss, p_rs, ya_ss, ya_rs, yb_ss, yb_rs, x_ss, x_rs, z_ss, z_rs, t_ss, t_rs,
):
    s = lax.axis_index("seq")
    y = lax.axis_index("dp")
    core = lax.rem(s, 2)
    x = lax.rem(s // 2, NX)
    z = s // (2 * NX)
    sib = s + 1 - 2 * core
    heads = range(HEADS)
    far = (2, 1)

    def ring(by):
        return lax.rem(s + by + N_SEQ, N_SEQ)

    def x_of(k):
        return lax.rem(x + k, NX)

    def at_x(k):
        return z * (2 * NX) + x_of(k) * 2 + core

    def at_z(m):
        return lax.rem(z + m, NZ) * (2 * NX) + x * 2 + core

    def at_y(j):
        return lax.rem(y + j, NY)

    barrier = pltpu.get_barrier_semaphore()

    def greet(seq, dp):
        pl.semaphore_signal(barrier, inc=1, device_id={"seq": seq, "dp": dp}, device_id_type=MESH)

    for by in (-2, -1, 1, 2):
        greet(ring(by), y)
    for j in range(1, NY):
        greet(s, at_y(j))
        greet(sib, at_y(j))
    for k in range(1, NX):
        greet(at_x(k), y)
    loop(NZ - 1, lambda m: greet(at_z(m + 1), y))

    def cols(h):
        return slice(h * HEAD_DIM, (h + 1) * HEAD_DIM)

    q_loads = [pltpu.make_async_copy(q_in.at[0, :, cols(h)], q3.at[h, 0], ld_sem.at[0, h]) for h in heads]
    k_loads = [pltpu.make_async_copy(k_in.at[0, :, cols(h)], kb.at[h], ld_sem.at[1, h]) for h in heads]
    v_loads = [pltpu.make_async_copy(v_in.at[0, :, cols(h)], vb.at[h], ld_sem.at[2, h]) for h in heads]
    gate_loads = [pltpu.make_async_copy(gate_in.at[0, :, cols(h)], gb.at[h], ld_sem.at[3, h]) for h in heads]
    og_loads = [
        pltpu.make_async_copy(og_in.at[0, :, cols(i)], ogb.at[i], ld_sem.at[4, i]) for i in range(2 * HEADS)
    ]
    w_load = pltpu.make_async_copy(w_in, wb, few_sem.at[0])
    few_loads = [pltpu.make_async_copy(len_in, len_ref, few_sem.at[1]), pltpu.make_async_copy(pat_in, pat_ref, few_sem.at[2])]
    for load in q_loads + k_loads + few_loads + v_loads + og_loads + [w_load] + gate_loads:
        load.start()

    def send(src, dst, ss, rs, seq, dp):
        return pltpu.make_async_remote_copy(
            src_ref=src, dst_ref=dst, send_sem=ss, recv_sem=rs,
            device_id={"seq": seq, "dp": dp}, device_id_type=MESH,
        )

    def rows_of(r):
        return pl.ds(r * PART, PART)

    def band_copy(src, dst, ss, rs, t, h, r, by):
        return send(src.at[rows_of(r)], dst.at[rows_of(r)], ss.at[t - 1, h, r], rs.at[t - 1, h, r], ring(by), y)

    def q_copy(t, h, r):
        return band_copy(q3.at[h, 0], q3.at[h, t], q_ss, q_rs, t, h, r, -t)

    def m_copy(t, h, r):
        return band_copy(ps.at[h, t - 1], mr.at[h, t - 1], m_ss, m_rs, t, h, r, t)

    def d_copy(t, h, r):
        return band_copy(dsend.at[h, t - 1], d3.at[h, t], d_ss, d_rs, t, h, r, -t)

    def e_copy(t, h, r):
        return band_copy(es.at[h, t - 1], er.at[h, t - 1], e_ss, e_rs, t, h, r, t)

    q_loads[0].wait()
    pl.semaphore_wait(barrier, 4 + 2 * (NY - 1) + (NX - 1) + (NZ - 1))
    for r in range(PARTS):
        for h in heads:
            if h and not r:
                q_loads[h].wait()
            for t in far:
                q_copy(t, h, r).start()

    for load in few_loads:
        load.wait()
    ends = []
    total = jnp.int32(0)
    for i in range(len_ref.shape[1]):
        total = total + len_ref[0, i]
        ends.append(total)

    def doc(at):
        number = jnp.zeros(at.shape, jnp.int32)
        for end in ends:
            number = number + jnp.where(at >= end, 1, 0)
        return number

    key_at = s * ROWS + lax.broadcasted_iota(jnp.int32, (1, ROWS), 1)
    key_doc = doc(key_at)
    for t in range(BAND + 1):
        query_at = (s + t) * ROWS + lax.broadcasted_iota(jnp.int32, (ROWS, 1), 0)
        keep = (doc(query_at) == key_doc) & (key_at <= query_at)
        mask[t] = jnp.where(keep, SCALE, 0.0).astype(F32)
        half[t] = jnp.where(keep, 0.5 * SCALE, 0.0).astype(F32)

    own = slice(0, 1)
    both = pl.ds(1, BAND)

    def flat(array):
        return array.reshape(-1, array.shape[-1])

    def forward(ts, rows, h):
        shape = (1 if ts is own else BAND, rows.size, ROWS)
        scores = dot_nt(flat(q3[h, ts, rows]), kb[h])
        middle = 0.5 * scores
        tanh = jnp.tanh(middle)
        twice = 1.0 + tanh
        silu = middle * twice
        a = (silu * flat(mask[ts, rows])).astype(BF16)
        attn[h, ts, rows] = a.reshape(shape)
        slope[h, ts, rows] = ((twice + silu * (1.0 - tanh)) * flat(half[ts, rows])).reshape(shape)
        return dot(a, vb[h])

    for load in k_loads + v_loads:
        load.wait()
    for h in heads:
        mix[h] = forward(own, pl.ds(0, ROWS), h)

    for load in og_loads:
        load.wait()
    w_load.wait()
    og = jnp.concatenate([ogb[i] for i in range(2 * HEADS)], axis=1)
    for i in range(2):
        part = dot_nt(og, wb[pl.ds(i * 256, 256), :])
        dgt[2 * i] = part[:, :HEAD_DIM]
        dgt[2 * i + 1] = part[:, HEAD_DIM:]
    for load in gate_loads:
        load.wait()

    def far_forward(h, r):
        for t in far:
            q_copy(t, h, r).wait_recv()
        ps[h, :, rows_of(r)] = forward(both, rows_of(r), h).astype(BF16).reshape(BAND, PART, HEAD_DIM)
        for t in far:
            m_copy(t, h, r).start()

    near = [jnp.where(pat_ref[0, 0, t] > 0, 1.0, 0.0).astype(F32) for t in range(BAND)]

    step_rows = 64

    def norm(rows):
        def mean(parts):
            return jnp.sum(sum(parts[1:], parts[0]), axis=1, keepdims=True) * (1.0 / WIDTH)

        mixed = [
            mix[h, rows] + near[0] * mr[h, 0, rows].astype(F32) + near[1] * mr[h, 1, rows].astype(F32) for h in heads
        ]
        centre = mean(mixed)
        mixed = [m - centre for m in mixed]
        inv = lax.rsqrt(mean([m * m for m in mixed]) + EPS)
        normed = [m * inv for m in mixed]
        grad = []
        gated = []
        for h in heads:
            gate = gb[h, rows].astype(F32)
            gated.append((normed[h] * gate).astype(BF16))
            up = dgt[h, rows]
            dgo[rows, cols(h)] = (up * normed[h]).astype(BF16)
            grad.append(up * gate)
        first = mean(grad)
        second = mean([g * n for g, n in zip(grad, normed)])
        for h in heads:
            down = (inv * (grad[h] - first - normed[h] * second)).astype(BF16)
            d3[h, 0, rows] = down
            for t in range(BAND):
                dsend[h, t, rows] = (near[t] * down.astype(F32)).astype(BF16)

        return jnp.concatenate(gated, axis=1)

    def norm_part(r):
        for h in heads:
            for t in far:
                m_copy(t, h, r).wait_recv()
        gated = [norm(pl.ds(r * PART + i * step_rows, step_rows)) for i in range(PART // step_rows)]
        for h in heads:
            for t in far:
                d_copy(t, h, r).start()
        gated = jnp.concatenate(gated, axis=0)
        gt[:, :, :, rows_of(r)] = gated.T.astype(F32).reshape(NZ, NX, 8, PART)

    def backward(ts, rows, h):
        q = flat(q3[h, ts, rows])
        d = flat(d3[h, ts, rows])
        ds = (dot_nt(d, vb[h]) * flat(slope[h, ts, rows])).astype(BF16)
        return dot(ds, kb[h]), dot_tn(ds, q), dot_tn(flat(attn[h, ts, rows]), d)

    def own_backward(r):
        for h in heads:
            dq, dk, dv = backward(own, rows_of(r), h)
            dqa[h, rows_of(r)] = dq
            dka[h] = dk if r == 0 else dka[h] + dk
            dva[h] = dv if r == 0 else dva[h] + dv

    def far_backward(h, r):
        for t in far:
            d_copy(t, h, r).wait_recv()
        dq, dk, dv = backward(both, rows_of(r), h)
        es[h, :, rows_of(r)] = dq.astype(BF16).reshape(BAND, PART, HEAD_DIM)
        for t in far:
            e_copy(t, h, r).start()
        if r < PARTS - 1:
            dka[h] = dka[h] + dk
            dva[h] = dva[h] + dv
        else:
            dko[:, cols(h)] = (dka[h] + dk).astype(BF16)
            dvo[:, cols(h)] = (dva[h] + dv).astype(BF16)

    for h in heads:
        far_forward(h, 0)
    far_forward(0, 1)
    far_forward(1, 1)
    norm_part(0)
    far_forward(2, 1)
    far_forward(3, 1)
    own_backward(0)
    norm_part(1)

    piece = NZ * 8
    cut = piece // 2
    low = slice(0, cut)
    high = slice(cut, piece)
    up = at_y(1)
    down = at_y(NY - 1)
    across = at_y(2)

    def p_copy(k):
        return send(gs.at[k], gr.at[k], p_ss.at[k], p_rs.at[k], sib, y)

    def ya_copy(k, i):
        return send(ya.at[k, i], yar.at[k, i], ya_ss.at[k, i], ya_rs.at[k, i], s, (up, down)[i])

    def yb_copy(k, i):
        return send(yb.at[k, i], ybr.at[k, i], yb_ss.at[k, i], yb_rs.at[k, i], s, (up, down)[i])

    def x_copy(k):
        return send(xs.at[k], xr.at[k], x_ss.at[k], x_rs.at[k], at_x(k), y)

    order = (2, 1, 3, 0)
    other = jnp.concatenate([ogb[(1 - core) * 4 + i] for i in range(NY)], axis=1)
    for k in order:
        part = dot(gt[:, x_of(k)].reshape(piece, ROWS).astype(BF16), other)
        for i in range(NY):
            gs[k, i] = part[:, cols(i)].astype(BF16)
        p_copy(k).start()
    mine = jnp.concatenate([ogb[core * 4 + i] for i in range(NY)], axis=1)
    for k in order:
        part = dot(gt[:, x_of(k)].reshape(piece, ROWS).astype(BF16), mine)
        for i in range(NY):
            gown[k, i] = part[:, cols(i)]

    for k in order:
        p_copy(k).wait_recv()
        for i in range(NY):
            gown[k, i] = gown[k, i] + gr[k, i].astype(F32)
        ya[k, 0] = gown[k, across, low].astype(BF16)
        ya[k, 1] = gown[k, across, high].astype(BF16)
        for i in range(2):
            ya_copy(k, i).start()

    def y_pass(k):
        for i in range(2):
            ya_copy(k, i).wait_recv()
        yb[k, 0, low] = (gown[k, up, low] + yar[k, 0].astype(F32)).astype(BF16)
        yb[k, 0, high] = gown[k, up, high].astype(BF16)
        yb[k, 1, low] = gown[k, down, low].astype(BF16)
        yb[k, 1, high] = (gown[k, down, high] + yar[k, 1].astype(F32)).astype(BF16)
        for i in range(2):
            yb_copy(k, i).start()

    gate_out = pltpu.make_async_copy(dgo, dg_out.at[0], out_sem.at[0])
    gate_out.start()

    def y_sum(k):
        for i in range(2):
            yb_copy(k, i).wait_recv()
        return gown[k, y] + ybr[k, 0].astype(F32) + ybr[k, 1].astype(F32)

    def x_start(k):
        xs[k] = y_sum(k).astype(BF16)
        x_copy(k).start()

    far_backward(0, 0)
    far_backward(1, 0)
    y_pass(2)
    y_pass(1)
    far_backward(2, 0)
    y_pass(3)
    y_pass(0)
    far_backward(3, 0)
    own_backward(1)
    x_start(2)
    far_backward(0, 1)
    x_start(1)
    far_backward(1, 1)
    x_start(3)

    z_order = (8, 7, 9, 6, 10, 5, 11, 4, 12, 3, 13, 2, 14, 1, 15)

    def z_copy(m):
        return send(zs.at[lax.rem(z + m, NZ)], zr.at[m], z_ss.at[m], z_rs.at[m], at_z(m), y)

    plane = y_sum(0)
    for k in range(1, NX):
        x_copy(k).wait_recv()
        plane = plane + xr[k].astype(F32)
    zs[...] = plane.reshape(NZ, 8, 128)
    for m in z_order:
        z_copy(m).start()

    far_backward(2, 1)
    far_backward(3, 1)
    key_out = pltpu.make_async_copy(dko, dk_out.at[0], out_sem.at[1])
    value_out = pltpu.make_async_copy(dvo, dv_out.at[0], out_sem.at[2])
    key_out.start()
    value_out.start()

    def t_copy(dy, dc):
        slot = core * NY + y
        seq = s if dc == 0 else sib
        return send(tiles.at[slot], tiles.at[slot], t_ss.at[dy * 2 + dc], t_rs.at[slot], seq, at_y(dy))

    others = [(dy, dc) for dy in range(NY) for dc in range(2) if (dy, dc) != (0, 0)]

    for m in z_order:
        z_copy(m).wait_recv()
    tile = zs[z]
    for m in range(1, NZ):
        tile = tile + zr[m]
    tiles[core * NY + y] = tile
    for dy, dc in others:
        t_copy(dy, dc).start()

    for h in heads:
        for r in range(PARTS):
            for t in far:
                e_copy(t, h, r).wait_recv()
        dqo[:, cols(h)] = (dqa[h] + er[h, 0].astype(F32) + er[h, 1].astype(F32)).astype(BF16)
    query_out = pltpu.make_async_copy(dqo, dq_out.at[0], out_sem.at[3])
    query_out.start()

    for dy, dc in others:
        slot = (core if dc == 0 else 1 - core) * NY + at_y(dy)
        send(tiles.at[slot], tiles.at[slot], t_ss.at[dy * 2 + dc], t_rs.at[slot], s, y).wait_recv()
    lower = jnp.broadcast_to(core, (4, 128)) == 0
    for slot in range(2 * NY):
        full = tiles[slot]
        wg_out[:, slot * 128:(slot + 1) * 128] = jnp.where(lower, full[:4], full[4:])

    for h in heads:
        for t in far:
            for r in range(PARTS):
                for copy in (q_copy, m_copy, d_copy, e_copy):
                    copy(t, h, r).wait_send()
    for k in range(NX):
        p_copy(k).wait_send()
        for i in range(2):
            ya_copy(k, i).wait_send()
            yb_copy(k, i).wait_send()
        if k:
            x_copy(k).wait_send()
    for m in z_order:
        z_copy(m).wait_send()
    for dy, dc in others:
        t_copy(dy, dc).wait_send()
    for out in (gate_out, key_out, value_out, query_out):
        out.wait()


def finish(*refs):
    sem = refs[-1]
    n = len(refs) // 2
    copies = [pltpu.make_async_copy(refs[i], refs[n + i], sem.at[i]) for i in range(n)]
    for copy in copies:
        copy.start()
    for copy in copies:
        copy.wait()


def finished(arrays):
    anywhere = pl.BlockSpec(memory_space=pl.ANY)
    return pl.pallas_call(
        finish,
        out_shape=tuple(jax.ShapeDtypeStruct(a.shape, a.dtype) for a in arrays),
        in_specs=[pl.BlockSpec(memory_space=pltpu.VMEM)] * len(arrays),
        out_specs=(anywhere,) * len(arrays),
        scratch_shapes=[pltpu.SemaphoreType.DMA((len(arrays),))],
        compiler_params=pltpu.CompilerParams(vmem_limit_bytes=16 * 1024 * 1024),
    )(*arrays)


def local(queries, keys, values, gates, out_weight, out_grad, lengths, pattern):
    block = (HEADS, ROWS, HEAD_DIM)
    two = (HEADS, BAND, ROWS, HEAD_DIM)
    three = (HEADS, BAND + 1, ROWS, HEAD_DIM)
    band = (BAND + 1, ROWS, ROWS)
    rows = (ROWS, WIDTH)
    vmem = pltpu.VMEM
    smem = pltpu.SMEM
    scratch = [
        smem(lengths.shape, jnp.int32), smem(pattern.shape, jnp.int32),
        vmem(three, BF16), vmem(block, BF16), vmem(block, BF16), vmem(block, BF16),
        vmem((2 * HEADS, ROWS, HEAD_DIM), BF16), vmem((WIDTH, MODEL), BF16),
        vmem(band, F32), vmem(band, F32), vmem(block, F32), vmem(block, F32),
        vmem(two, BF16), vmem(two, BF16),
        vmem(three, BF16), vmem(two, BF16), vmem(two, BF16), vmem(two, BF16),
        vmem((HEADS,) + band, BF16), vmem((HEADS,) + band, F32),
        vmem((NZ, NX, 8, ROWS), F32),
        vmem((NX, NY, NZ * 8, 128), F32), vmem((NX, NY, NZ * 8, 128), BF16), vmem((NX, NY, NZ * 8, 128), BF16),
        vmem((NX, 2, NZ * 4, 128), BF16), vmem((NX, 2, NZ * 4, 128), BF16),
        vmem((NX, 2, NZ * 8, 128), BF16), vmem((NX, 2, NZ * 8, 128), BF16),
        vmem((NX, NZ * 8, 128), BF16), vmem((NX, NZ * 8, 128), BF16),
        vmem((NZ, 8, 128), F32), vmem((NZ, 8, 128), F32), vmem((2 * NY, 8, 128), F32),
        vmem(block, F32), vmem(block, F32), vmem(block, F32),
        vmem(rows, BF16), vmem(rows, BF16), vmem(rows, BF16), vmem(rows, BF16),
    ]
    dma = pltpu.SemaphoreType.DMA
    scratch += [dma((5, 2 * HEADS)), dma((3,)), dma((4,))]
    scratch += [dma((BAND, HEADS, PARTS))] * 8
    scratch += [dma((NX,))] * 2 + [dma((NX, 2))] * 4 + [dma((NX,))] * 2 + [dma((NZ,))] * 2 + [dma((2 * NY,))] * 2
    anywhere = pl.BlockSpec(memory_space=pl.ANY)
    grad = jax.ShapeDtypeStruct((1, ROWS, WIDTH), BF16)
    operands = (lengths, pattern, queries, keys, values, gates, out_weight, out_grad)
    results = pl.pallas_call(
        kernel,
        out_shape=(grad, grad, grad, grad, jax.ShapeDtypeStruct((WIDTH // N_SEQ, MODEL), F32)),
        in_specs=[anywhere] * len(operands),
        out_specs=(anywhere,) * 4 + (pl.BlockSpec(memory_space=pltpu.VMEM),),
        scratch_shapes=scratch,
        compiler_params=pltpu.CompilerParams(
            collective_id=0, has_side_effects=True, vmem_limit_bytes=40 * 1024 * 1024
        ),
        cost_estimate=pl.CostEstimate(flops=2 * 10**9, bytes_accessed=5 * 2**20, transcendentals=3 * 4 * ROWS * ROWS),
    )(*[pltpu.with_memory_space_constraint(a, pltpu.HBM) for a in operands])
    return finished(results)


def solution(mesh):
    events = P("dp", "seq", None)
    return jax.shard_map(
        local,
        mesh=mesh,
        in_specs=(events, events, events, events, P(), events, P("dp", None), events),
        out_specs=(events, events, events, events, P("seq", None)),
        check_vma=False,
    )
```

```python
import jax
import jax.numpy as jnp
from jax import lax
from jax.experimental import pallas as pl
from jax.experimental.pallas import tpu as pltpu
from jax.sharding import PartitionSpec as P

MESH = pl.DeviceIdType.MESH
EPS = 1e-05
HEADS = 4
HEAD_DIM = 128
ROWS = 256
WIDTH = 512
MODEL = 1024
NX = 4
NZ = 16
NY = 4
N_SEQ = 128
BAND = 2
PARTS = 2
PART = ROWS // PARTS
SCALE = 1.0 / ((BAND + 1) * ROWS)
BF16 = jnp.bfloat16
F32 = jnp.float32
NT = (((1,), (1,)), ((), ()))
TN = (((0,), (0,)), ((), ()))


def dot(a, b):
    return jnp.dot(a, b, preferred_element_type=F32)


def dot_nt(a, b):
    return lax.dot_general(a, b, NT, preferred_element_type=F32)


def dot_tn(a, b):
    return lax.dot_general(a, b, TN, preferred_element_type=F32)


def loop(n, body):
    lax.fori_loop(0, n, lambda i, c: (body(i), c)[1], jnp.int32(0))


def kernel(
    len_in, pat_in, q_in, k_in, v_in, gate_in, w_in, og_in,
    dq_out, dk_out, dv_out, dg_out, wg_out,
    len_ref, pat_ref, q3, kb, vb, gb, ogb, wb, kt, vt, mask, half, dgt, mix,
    ps, mr, d3, dsend, es, er, attn_own, attn_far, qt_own, qt_far, slope_own, slope_far, gt,
    gown, gs, gr, ya, yar, yb, ybr, xs, xr, zs, zr, tiles,
    dqa, dka, dva, dqo, dko, dvo, dgo,
    ld_sem, out_sem, q_ss, q_rs, m_ss, m_rs, d_ss, d_rs, e_ss, e_rs,
    p_ss, p_rs, ya_ss, ya_rs, yb_ss, yb_rs, x_ss, x_rs, z_ss, z_rs, t_ss, t_rs,
):
    s = lax.axis_index("seq")
    y = lax.axis_index("dp")
    core = lax.rem(s, 2)
    x = lax.rem(s // 2, NX)
    z = s // (2 * NX)
    sib = s + 1 - 2 * core
    heads = range(HEADS)
    far = (2, 1)

    def ring(by):
        return lax.rem(s + by + N_SEQ, N_SEQ)

    def x_of(k):
        return lax.rem(x + k, NX)

    def at_x(k):
        return z * (2 * NX) + x_of(k) * 2 + core

    def at_z(m):
        return lax.rem(z + m, NZ) * (2 * NX) + x * 2 + core

    def at_y(j):
        return lax.rem(y + j, NY)

    barrier = pltpu.get_barrier_semaphore()

    def greet(seq, dp):
        pl.semaphore_signal(barrier, inc=1, device_id={"seq": seq, "dp": dp}, device_id_type=MESH)

    def cols(h):
        return slice(h * HEAD_DIM, (h + 1) * HEAD_DIM)

    for by in (-2, -1, 1, 2):
        greet(ring(by), y)
    q_loads = [pltpu.make_async_copy(q_in.at[0, :, cols(h)], q3.at[h, 0], ld_sem.at[h]) for h in heads]
    for load in q_loads:
        load.start()
    for j in range(1, NY):
        greet(s, at_y(j))
        greet(sib, at_y(j))
    for k in range(1, NX):
        greet(at_x(k), y)
    for m in range(1, NZ):
        greet(at_z(m), y)

    k_load = pltpu.make_async_copy(k_in.at[0], kb, ld_sem.at[4])
    v_load = pltpu.make_async_copy(v_in.at[0], vb, ld_sem.at[5])
    gate_load = pltpu.make_async_copy(gate_in.at[0], gb, ld_sem.at[6])
    og_load = pltpu.make_async_copy(og_in.at[0], ogb, ld_sem.at[7])
    w_load = pltpu.make_async_copy(w_in, wb, ld_sem.at[8])
    few_loads = [pltpu.make_async_copy(len_in, len_ref, ld_sem.at[9]), pltpu.make_async_copy(pat_in, pat_ref, ld_sem.at[10])]
    for load in [k_load, v_load] + few_loads + [og_load, w_load, gate_load]:
        load.start()

    def send(src, dst, ss, rs, seq, dp):
        return pltpu.make_async_remote_copy(
            src_ref=src, dst_ref=dst, send_sem=ss, recv_sem=rs,
            device_id={"seq": seq, "dp": dp}, device_id_type=MESH,
        )

    def rows_of(r):
        return pl.ds(r * PART, PART)

    def band_copy(src, dst, ss, rs, h, r, by):
        return send(src.at[rows_of(r)], dst.at[rows_of(r)], ss.at[0], rs, ring(by), y)

    def q_copy(t, h, r):
        return band_copy(q3.at[h, 0], q3.at[h, t], q_ss, q_rs.at[h, r], h, r, -t)

    def m_copy(t, h, r):
        return band_copy(ps.at[h, t - 1], mr.at[h, t - 1], m_ss, m_rs.at[r], h, r, t)

    def d_copy(t, h, r):
        return band_copy(dsend.at[h, t - 1], d3.at[h, t], d_ss, d_rs.at[h, r], h, r, -t)

    def e_copy(t, h, r):
        return band_copy(es.at[h, t - 1], er.at[h, t - 1], e_ss, e_rs.at[0], h, r, t)

    def landed(ref, sem):
        send(ref, ref, sem, sem, sib, y).wait_recv()

    def sent(ref, sem):
        send(ref, ref, sem, sem, sib, y).wait_send()

    q_loads[0].wait()
    pl.semaphore_wait(barrier, 4 + 2 * (NY - 1) + (NX - 1) + (NZ - 1))
    for r in range(PARTS):
        for h in heads:
            if h and not r:
                q_loads[h].wait()
            for t in far:
                q_copy(t, h, r).start()

    for load in few_loads:
        load.wait()
    ends = []
    total = jnp.int32(0)
    for i in range(len_ref.shape[1]):
        total = total + len_ref[0, i]
        ends.append(total)

    def doc(at):
        number = jnp.zeros(at.shape, jnp.int32)
        for end in ends:
            number = number + jnp.where(at >= end, 1, 0)
        return number

    key_at = s * ROWS + lax.broadcasted_iota(jnp.int32, (1, ROWS), 1)
    key_doc = doc(key_at)
    for t in range(BAND + 1):
        query_at = (s + t) * ROWS + lax.broadcasted_iota(jnp.int32, (ROWS, 1), 0)
        keep = (doc(query_at) == key_doc) & (key_at <= query_at)
        mask[t] = jnp.where(keep, SCALE, 0.0).astype(F32)
        half[t] = jnp.where(keep, 0.5 * SCALE, 0.0).astype(F32)

    own = slice(0, 1)
    both = pl.ds(1, BAND)

    def flat(array):
        return array.reshape(-1, array.shape[-1])

    def forward(ts, rows, h):
        q = flat(q3[h, ts, rows])
        scores = dot(q, kt[h])
        middle = 0.5 * scores
        tanh = jnp.tanh(middle)
        twice = 1.0 + tanh
        silu = middle * twice
        a = (silu * flat(mask[ts, rows])).astype(BF16)
        slope = (twice + silu * (1.0 - tanh)) * flat(half[ts, rows])
        return q, a, slope, dot(a, vb[:, cols(h)])

    k_load.wait()
    for h in heads:
        kt[h] = kb[:, cols(h)].T
    v_load.wait()
    for h in heads:
        vt[h] = vb[:, cols(h)].T
    for h in heads:
        q, a, slope_own[h], mix[h] = forward(own, pl.ds(0, ROWS), h)
        attn_own[h] = a.T
        qt_own[h] = q.T

    og_load.wait()
    w_load.wait()
    og = ogb[...]
    for i in range(2):
        part = dot_nt(og, wb[pl.ds(i * 256, 256), :])
        dgt[2 * i] = part[:, :HEAD_DIM]
        dgt[2 * i + 1] = part[:, HEAD_DIM:]
    gate_load.wait()

    def far_forward(h, r):
        landed(q3.at[h, both, rows_of(r)], q_rs.at[h, r])
        q, a, slope_far[h, r], part = forward(both, rows_of(r), h)
        ps[h, :, rows_of(r)] = part.astype(BF16).reshape(BAND, PART, HEAD_DIM)
        for t in far:
            m_copy(t, h, r).start()
        attn_far[h, r] = a.T
        qt_far[h, r] = q.T

    near = [jnp.where(pat_ref[0, 0, t] > 0, 1.0, 0.0).astype(F32) for t in range(BAND)]

    step_rows = 64

    def norm(rows):
        def mean(parts):
            return jnp.sum(sum(parts[1:], parts[0]), axis=1, keepdims=True) * (1.0 / WIDTH)

        mixed = [
            mix[h, rows] + near[0] * mr[h, 0, rows].astype(F32) + near[1] * mr[h, 1, rows].astype(F32) for h in heads
        ]
        centre = mean(mixed)
        mixed = [m - centre for m in mixed]
        inv = lax.rsqrt(mean([m * m for m in mixed]) + EPS)
        normed = [m * inv for m in mixed]
        grad = []
        gated = []
        for h in heads:
            gate = gb[rows, cols(h)].astype(F32)
            gated.append((normed[h] * gate).astype(BF16))
            up = dgt[h, rows]
            dgo[rows, cols(h)] = (up * normed[h]).astype(BF16)
            grad.append(up * gate)
        first = mean(grad)
        second = mean([g * n for g, n in zip(grad, normed)])
        for h in heads:
            down = (inv * (grad[h] - first - normed[h] * second)).astype(BF16)
            d3[h, 0, rows] = down
            for t in range(BAND):
                dsend[h, t, rows] = (near[t] * down.astype(F32)).astype(BF16)

        return jnp.concatenate(gated, axis=1)

    def norm_part(r):
        landed(mr.at[:, :, rows_of(r)], m_rs.at[r])
        gated = [norm(pl.ds(r * PART + i * step_rows, step_rows)) for i in range(PART // step_rows)]
        for h in heads:
            for t in far:
                d_copy(t, h, r).start()
        gated = jnp.concatenate(gated, axis=0)
        gt[:, :, :, rows_of(r)] = gated.T.astype(F32).reshape(NZ, NX, 8, PART)

    def backward(d, slope, h, q_t, attn_t):
        ds = (dot(d, vt[h]) * slope).astype(BF16)
        return dot(ds, kb[:, cols(h)]), dot(q_t, ds), dot(attn_t, d)

    def own_backward(r):
        lanes = slice(r * PART, (r + 1) * PART)
        for h in heads:
            dq, dk, dv = backward(d3[h, 0, rows_of(r)], slope_own[h, rows_of(r)], h, qt_own[h, :, lanes], attn_own[h, :, lanes])
            dqa[h, rows_of(r)] = dq
            dka[h] = dk if r == 0 else dka[h] + dk
            dva[h] = dv if r == 0 else dva[h] + dv

    def far_backward(h, r):
        landed(d3.at[h, both, rows_of(r)], d_rs.at[h, r])
        dq, dk, dv = backward(flat(d3[h, both, rows_of(r)]), slope_far[h, r], h, qt_far[h, r], attn_far[h, r])
        es[h, :, rows_of(r)] = dq.astype(BF16).reshape(BAND, PART, HEAD_DIM)
        for t in far:
            e_copy(t, h, r).start()
        if r < PARTS - 1:
            dka[h] = dka[h] + dk
            dva[h] = dva[h] + dv
        else:
            dko[:, cols(h)] = (dka[h] + dk).T.astype(BF16)
            dvo[:, cols(h)] = (dva[h] + dv).astype(BF16)

    for h in heads:
        far_forward(h, 0)
    far_forward(0, 1)
    far_forward(1, 1)
    norm_part(0)
    far_forward(2, 1)
    far_forward(3, 1)
    own_backward(0)
    norm_part(1)

    piece = NZ * 8
    cut = piece // 2
    low = slice(0, cut)
    high = slice(cut, piece)
    up = at_y(1)
    down = at_y(NY - 1)
    across = at_y(2)

    def p_copy(k):
        return send(gs.at[k], gr.at[k], p_ss.at[0], p_rs.at[k], sib, y)

    def ya_copy(k, i):
        return send(ya.at[k, i], yar.at[k, i], ya_ss.at[0], ya_rs.at[k], s, (up, down)[i])

    def yb_copy(k, i):
        return send(yb.at[k, i], ybr.at[k, i], yb_ss.at[0], yb_rs.at[k], s, (up, down)[i])

    def x_copy(k):
        return send(xs.at[k], xr.at[k], x_ss.at[0], x_rs.at[0], at_x(k), y)

    order = (2, 1, 3, 0)
    other = ogb[:, pl.ds(pl.multiple_of((1 - core) * WIDTH, WIDTH), WIDTH)]
    for k in order:
        part = dot(gt[:, x_of(k)].reshape(piece, ROWS).astype(BF16), other)
        for i in range(NY):
            gs[k, i] = part[:, cols(i)].astype(BF16)
        p_copy(k).start()
    mine = ogb[:, pl.ds(pl.multiple_of(core * WIDTH, WIDTH), WIDTH)]
    for k in order:
        part = dot(gt[:, x_of(k)].reshape(piece, ROWS).astype(BF16), mine)
        for i in range(NY):
            gown[k, i] = part[:, cols(i)]

    for k in order:
        p_copy(k).wait_recv()
        for i in range(NY):
            gown[k, i] = gown[k, i] + gr[k, i].astype(F32)
        ya[k, 0] = gown[k, across, low].astype(BF16)
        ya[k, 1] = gown[k, across, high].astype(BF16)
        for i in range(2):
            ya_copy(k, i).start()

    def y_pass(k):
        landed(yar.at[k], ya_rs.at[k])
        yb[k, 0, low] = (gown[k, up, low] + yar[k, 0].astype(F32)).astype(BF16)
        yb[k, 0, high] = gown[k, up, high].astype(BF16)
        yb[k, 1, low] = gown[k, down, low].astype(BF16)
        yb[k, 1, high] = (gown[k, down, high] + yar[k, 1].astype(F32)).astype(BF16)
        for i in range(2):
            yb_copy(k, i).start()

    gate_out = pltpu.make_async_copy(dgo, dg_out.at[0], out_sem.at[0])
    gate_out.start()

    def y_sum(k):
        landed(ybr.at[k], yb_rs.at[k])
        return gown[k, y] + ybr[k, 0].astype(F32) + ybr[k, 1].astype(F32)

    def x_start(k):
        xs[k] = y_sum(k).astype(BF16)
        x_copy(k).start()

    far_backward(0, 0)
    far_backward(1, 0)
    y_pass(2)
    y_pass(1)
    far_backward(2, 0)
    y_pass(3)
    y_pass(0)
    far_backward(3, 0)
    own_backward(1)
    x_start(2)
    far_backward(0, 1)
    x_start(1)
    far_backward(1, 1)
    x_start(3)

    z_order = (8, 7, 9, 6, 10, 5, 11, 4, 12, 3, 13, 2, 14, 1, 15)

    def z_copy(m):
        return send(zs.at[lax.rem(z + m, NZ)], zr.at[m], z_ss.at[0], z_rs.at[0], at_z(m), y)

    plane = y_sum(0)
    landed(xr.at[pl.ds(1, NX - 1)], x_rs.at[0])
    for k in range(1, NX):
        plane = plane + xr[k].astype(F32)
    zs[...] = plane.reshape(NZ, 8, 128)
    for m in z_order:
        z_copy(m).start()

    far_backward(2, 1)
    far_backward(3, 1)
    key_out = pltpu.make_async_copy(dko, dk_out.at[0], out_sem.at[1])
    value_out = pltpu.make_async_copy(dvo, dv_out.at[0], out_sem.at[2])
    key_out.start()
    value_out.start()

    def t_copy(dy, dc):
        slot = core * NY + y
        seq = s if dc == 0 else sib
        return send(tiles.at[slot], tiles.at[slot], t_ss.at[0], t_rs.at[0], seq, at_y(dy))

    others = [(dy, dc) for dy in range(NY) for dc in range(2) if (dy, dc) != (0, 0)]

    landed(zr.at[pl.ds(1, NZ - 1)], z_rs.at[0])
    tile = zs[z]
    for m in range(1, NZ):
        tile = tile + zr[m]
    tiles[core * NY + y] = tile
    for dy, dc in others:
        t_copy(dy, dc).start()

    landed(er, e_rs.at[0])
    for h in heads:
        dqo[:, cols(h)] = (dqa[h] + er[h, 0].astype(F32) + er[h, 1].astype(F32)).astype(BF16)
    query_out = pltpu.make_async_copy(dqo, dq_out.at[0], out_sem.at[3])
    query_out.start()

    for ref, sem in (
        (ps, q_ss), (ps, m_ss), (dsend, d_ss), (es, e_ss), (gs, p_ss), (ya, ya_ss), (yb, yb_ss),
        (xs.at[pl.ds(1, NX - 1)], x_ss), (zs.at[pl.ds(0, NZ - 1)], z_ss),
    ):
        sent(ref, sem.at[0])
    for out in (gate_out, key_out, value_out, query_out):
        out.wait()

    arrived = tiles.at[pl.ds(0, 2 * NY - 1)]
    landed(arrived, t_rs.at[0])
    lower = jnp.broadcast_to(core, (4, 128)) == 0
    for slot in range(2 * NY):
        full = tiles[slot]
        wg_out[:, slot * 128:(slot + 1) * 128] = jnp.where(lower, full[:4], full[4:])
    sent(arrived, t_ss.at[0])


def finish(*refs):
    sem = refs[-1]
    n = len(refs) // 2
    copies = [pltpu.make_async_copy(refs[i], refs[n + i], sem.at[i]) for i in range(n)]
    for copy in copies:
        copy.start()
    for copy in copies:
        copy.wait()


def finished(arrays):
    anywhere = pl.BlockSpec(memory_space=pl.ANY)
    return pl.pallas_call(
        finish,
        out_shape=tuple(jax.ShapeDtypeStruct(a.shape, a.dtype) for a in arrays),
        in_specs=[pl.BlockSpec(memory_space=pltpu.VMEM)] * len(arrays),
        out_specs=(anywhere,) * len(arrays),
        scratch_shapes=[pltpu.SemaphoreType.DMA((len(arrays),))],
        compiler_params=pltpu.CompilerParams(vmem_limit_bytes=16 * 1024 * 1024),
    )(*arrays)


def local(queries, keys, values, gates, out_weight, out_grad, lengths, pattern):
    block = (HEADS, ROWS, HEAD_DIM)
    block_t = (HEADS, HEAD_DIM, ROWS)
    two = (HEADS, BAND, ROWS, HEAD_DIM)
    three = (HEADS, BAND + 1, ROWS, HEAD_DIM)
    band = (BAND + 1, ROWS, ROWS)
    rows = (ROWS, WIDTH)
    vmem = pltpu.VMEM
    smem = pltpu.SMEM
    scratch = [
        smem(lengths.shape, jnp.int32), smem(pattern.shape, jnp.int32),
        vmem(three, BF16), vmem(rows, BF16), vmem(rows, BF16), vmem(rows, BF16),
        vmem((ROWS, MODEL), BF16), vmem((WIDTH, MODEL), BF16),
        vmem(block_t, BF16), vmem(block_t, BF16),
        vmem(band, F32), vmem(band, F32), vmem(block, F32), vmem(block, F32),
        vmem(two, BF16), vmem(two, BF16),
        vmem(three, BF16), vmem(two, BF16), vmem(two, BF16), vmem(two, BF16),
        vmem((HEADS, ROWS, ROWS), BF16), vmem((HEADS, PARTS, ROWS, BAND * PART), BF16),
        vmem(block_t, BF16), vmem((HEADS, PARTS, HEAD_DIM, BAND * PART), BF16),
        vmem((HEADS, ROWS, ROWS), F32), vmem((HEADS, PARTS, BAND * PART, ROWS), F32),
        vmem((NZ, NX, 8, ROWS), F32),
        vmem((NX, NY, NZ * 8, 128), F32), vmem((NX, NY, NZ * 8, 128), BF16), vmem((NX, NY, NZ * 8, 128), BF16),
        vmem((NX, 2, NZ * 4, 128), BF16), vmem((NX, 2, NZ * 4, 128), BF16),
        vmem((NX, 2, NZ * 8, 128), BF16), vmem((NX, 2, NZ * 8, 128), BF16),
        vmem((NX, NZ * 8, 128), BF16), vmem((NX, NZ * 8, 128), BF16),
        vmem((NZ, 8, 128), F32), vmem((NZ, 8, 128), F32), vmem((2 * NY, 8, 128), F32),
        vmem(block, F32), vmem(block_t, F32), vmem(block, F32),
        vmem(rows, BF16), vmem(rows, BF16), vmem(rows, BF16), vmem(rows, BF16),
    ]
    dma = pltpu.SemaphoreType.DMA
    one = dma((1,))
    scratch += [dma((11,)), dma((4,))]
    scratch += [one, dma((HEADS, PARTS)), one, dma((PARTS,)), one, dma((HEADS, PARTS)), one, one]
    scratch += [one, dma((NX,)), one, dma((NX,)), one, dma((NX,))]
    scratch += [one] * 6
    anywhere = pl.BlockSpec(memory_space=pl.ANY)
    grad = jax.ShapeDtypeStruct((1, ROWS, WIDTH), BF16)
    operands = (lengths, pattern, queries, keys, values, gates, out_weight, out_grad)
    results = pl.pallas_call(
        kernel,
        out_shape=(grad, grad, grad, grad, jax.ShapeDtypeStruct((WIDTH // N_SEQ, MODEL), F32)),
        in_specs=[anywhere] * len(operands),
        out_specs=(anywhere,) * 4 + (pl.BlockSpec(memory_space=pltpu.VMEM),),
        scratch_shapes=scratch,
        compiler_params=pltpu.CompilerParams(
            collective_id=0, has_side_effects=True, vmem_limit_bytes=40 * 1024 * 1024
        ),
        cost_estimate=pl.CostEstimate(flops=2 * 10**9, bytes_accessed=5 * 2**20, transcendentals=3 * 4 * ROWS * ROWS),
    )(*[pltpu.with_memory_space_constraint(a, pltpu.HBM) for a in operands])
    return finished(results)


def solution(mesh):
    events = P("dp", "seq", None)
    return jax.shard_map(
        local,
        mesh=mesh,
        in_specs=(events, events, events, events, P(), events, P("dp", None), events),
        out_specs=(events, events, events, events, P("seq", None)),
        check_vma=False,
    )
```

```python
import jax
import jax.numpy as jnp
from jax import lax
from jax.experimental import pallas as pl
from jax.experimental.pallas import tpu as pltpu
from jax.sharding import PartitionSpec as P

MESH = pl.DeviceIdType.MESH
EPS = 1e-05
HEADS = 4
HEAD_DIM = 128
ROWS = 256
WIDTH = 512
MODEL = 1024
NX = 4
NZ = 16
NY = 4
N_SEQ = 128
BAND = 2
PARTS = 2
PART = ROWS // PARTS
SCALE = 1.0 / ((BAND + 1) * ROWS)
BF16 = jnp.bfloat16
F32 = jnp.float32
NT = (((1,), (1,)), ((), ()))
TN = (((0,), (0,)), ((), ()))


def dot(a, b):
    return jnp.dot(a, b, preferred_element_type=F32)


def dot_nt(a, b):
    return lax.dot_general(a, b, NT, preferred_element_type=F32)


def dot_tn(a, b):
    return lax.dot_general(a, b, TN, preferred_element_type=F32)


def loop(n, body):
    lax.fori_loop(0, n, lambda i, c: (body(i), c)[1], jnp.int32(0))


def kernel(
    len_in, pat_in, q_in, k_in, v_in, gate_in, w_in, og_in,
    dq_out, dk_out, dv_out, dg_out, wg_out,
    len_ref, pat_ref, q3, kb, vb, gb, ogb, ogs, wb, kt, vt, mask, half, dgt, mix,
    ps, mr, d3, dsend, es, er, attn_own, attn_far, qt_own, qt_far, slope_own, slope_far, gt, gtb, gtr,
    gown, ya, yar, yb, ybr, xs, xr, zs, zr, tiles,
    dqa, dka, dva, dqo, dko, dvo, dgo,
    ld_sem, out_sem, q_ss, q_rs, m_ss, m_rs, d_ss, d_rs, e_ss, e_rs,
    o_ss, o_rs, g_ss, g_rs, ya_ss, ya_rs, yb_ss, yb_rs, x_ss, x_rs, z_ss, z_rs, t_ss, t_rs,
):
    s = lax.axis_index("seq")
    y = lax.axis_index("dp")
    core = lax.rem(s, 2)
    x = lax.rem(s // 2, NX)
    z = s // (2 * NX)
    sib = s + 1 - 2 * core
    heads = range(HEADS)
    far = (2, 1)

    def ring(by):
        return lax.rem(s + by + N_SEQ, N_SEQ)

    def x_of(k):
        return lax.rem(x + k, NX)

    def at_x(k):
        return z * (2 * NX) + x_of(k) * 2 + core

    def at_z(m):
        return lax.rem(z + m, NZ) * (2 * NX) + x * 2 + core

    def at_y(j):
        return lax.rem(y + j, NY)

    barrier = pltpu.get_barrier_semaphore()

    def greet(seq, dp):
        pl.semaphore_signal(barrier, inc=1, device_id={"seq": seq, "dp": dp}, device_id_type=MESH)

    def cols(h):
        return slice(h * HEAD_DIM, (h + 1) * HEAD_DIM)

    for by in (-2, -1, 1, 2):
        greet(ring(by), y)
    q_loads = [pltpu.make_async_copy(q_in.at[0, :, cols(h)], q3.at[h, 0], ld_sem.at[h]) for h in heads]
    for load in q_loads:
        load.start()
    for j in range(1, NY):
        greet(s, at_y(j))
        greet(sib, at_y(j))
    for k in range(1, NX):
        greet(at_x(k), y)
    for m in range(1, NZ):
        greet(at_z(m), y)

    k_load = pltpu.make_async_copy(k_in.at[0], kb, ld_sem.at[4])
    v_load = pltpu.make_async_copy(v_in.at[0], vb, ld_sem.at[5])
    gate_load = pltpu.make_async_copy(gate_in.at[0], gb, ld_sem.at[6])
    og_loads = [pltpu.make_async_copy(og_in.at[0, :, c * WIDTH:(c + 1) * WIDTH], ogb.at[c], ld_sem.at[11 + c]) for c in range(2)]
    w_load = pltpu.make_async_copy(w_in, wb, ld_sem.at[8])
    few_loads = [pltpu.make_async_copy(len_in, len_ref, ld_sem.at[9]), pltpu.make_async_copy(pat_in, pat_ref, ld_sem.at[10])]
    for load in [k_load, v_load] + few_loads + og_loads + [w_load, gate_load]:
        load.start()

    def send(src, dst, ss, rs, seq, dp):
        return pltpu.make_async_remote_copy(
            src_ref=src, dst_ref=dst, send_sem=ss, recv_sem=rs,
            device_id={"seq": seq, "dp": dp}, device_id_type=MESH,
        )

    def rows_of(r):
        return pl.ds(r * PART, PART)

    def band_copy(src, dst, ss, rs, h, r, by):
        return send(src.at[rows_of(r)], dst.at[rows_of(r)], ss.at[0], rs, ring(by), y)

    def q_copy(t, h, r):
        return band_copy(q3.at[h, 0], q3.at[h, t], q_ss, q_rs.at[h, r], h, r, -t)

    def m_copy(t, h, r):
        return band_copy(ps.at[h, t - 1], mr.at[h, t - 1], m_ss, m_rs.at[r], h, r, t)

    def d_copy(t, h, r):
        return band_copy(dsend.at[h, t - 1], d3.at[h, t], d_ss, d_rs.at[h, r], h, r, -t)

    def e_copy(t, h, r):
        return band_copy(es.at[h, t - 1], er.at[h, t - 1], e_ss, e_rs.at[0], h, r, t)

    def landed(ref, sem):
        send(ref, ref, sem, sem, sib, y).wait_recv()

    def sent(ref, sem):
        send(ref, ref, sem, sem, sib, y).wait_send()

    q_loads[0].wait()
    pl.semaphore_wait(barrier, 4 + 2 * (NY - 1) + (NX - 1) + (NZ - 1))
    for r in range(PARTS):
        for h in heads:
            if h and not r:
                q_loads[h].wait()
            for t in far:
                q_copy(t, h, r).start()

    for load in few_loads:
        load.wait()
    ends = []
    total = jnp.int32(0)
    for i in range(len_ref.shape[1]):
        total = total + len_ref[0, i]
        ends.append(total)

    def doc(at):
        number = jnp.zeros(at.shape, jnp.int32)
        for end in ends:
            number = number + jnp.where(at >= end, 1, 0)
        return number

    key_at = s * ROWS + lax.broadcasted_iota(jnp.int32, (1, ROWS), 1)
    key_doc = doc(key_at)
    for t in range(BAND + 1):
        query_at = (s + t) * ROWS + lax.broadcasted_iota(jnp.int32, (ROWS, 1), 0)
        keep = (doc(query_at) == key_doc) & (key_at <= query_at)
        mask[t] = jnp.where(keep, SCALE, 0.0).astype(F32)
        half[t] = jnp.where(keep, 0.5 * SCALE, 0.0).astype(F32)

    own = slice(0, 1)
    both = pl.ds(1, BAND)

    def flat(array):
        return array.reshape(-1, array.shape[-1])

    def forward(ts, rows, h):
        q = flat(q3[h, ts, rows])
        scores = dot(q, kt[h])
        middle = 0.5 * scores
        tanh = jnp.tanh(middle)
        twice = 1.0 + tanh
        silu = middle * twice
        a = (silu * flat(mask[ts, rows])).astype(BF16)
        slope = (twice + silu * (1.0 - tanh)) * flat(half[ts, rows])
        return q, a, slope, dot(a, vb[:, cols(h)])

    k_load.wait()
    for h in heads:
        kt[h] = kb[:, cols(h)].T
    v_load.wait()
    for h in heads:
        vt[h] = vb[:, cols(h)].T
    for h in heads:
        q, a, slope_own[h], mix[h] = forward(own, pl.ds(0, ROWS), h)
        attn_own[h] = a.T
        qt_own[h] = q.T

    for load in og_loads:
        load.wait()
    swap = send(ogb.at[1 - core], ogs, o_ss.at[0], o_rs.at[0], sib, y)
    swap.start()
    w_load.wait()
    og = jnp.concatenate([ogb[0], ogb[1]], axis=1)
    for i in range(2):
        part = dot_nt(og, wb[pl.ds(i * 256, 256), :])
        dgt[2 * i] = part[:, :HEAD_DIM]
        dgt[2 * i + 1] = part[:, HEAD_DIM:]
    gate_load.wait()

    def far_forward(h, r):
        landed(q3.at[h, both, rows_of(r)], q_rs.at[h, r])
        q, a, slope_far[h, r], part = forward(both, rows_of(r), h)
        ps[h, :, rows_of(r)] = part.astype(BF16).reshape(BAND, PART, HEAD_DIM)
        for t in far:
            m_copy(t, h, r).start()
        attn_far[h, r] = a.T
        qt_far[h, r] = q.T

    near = [jnp.where(pat_ref[0, 0, t] > 0, 1.0, 0.0).astype(F32) for t in range(BAND)]

    step_rows = 64

    def norm(rows):
        def mean(parts):
            return jnp.sum(sum(parts[1:], parts[0]), axis=1, keepdims=True) * (1.0 / WIDTH)

        mixed = [
            mix[h, rows] + near[0] * mr[h, 0, rows].astype(F32) + near[1] * mr[h, 1, rows].astype(F32) for h in heads
        ]
        centre = mean(mixed)
        mixed = [m - centre for m in mixed]
        inv = lax.rsqrt(mean([m * m for m in mixed]) + EPS)
        normed = [m * inv for m in mixed]
        grad = []
        gated = []
        for h in heads:
            gate = gb[rows, cols(h)].astype(F32)
            gated.append((normed[h] * gate).astype(BF16))
            up = dgt[h, rows]
            dgo[rows, cols(h)] = (up * normed[h]).astype(BF16)
            grad.append(up * gate)
        first = mean(grad)
        second = mean([g * n for g, n in zip(grad, normed)])
        for h in heads:
            down = (inv * (grad[h] - first - normed[h] * second)).astype(BF16)
            d3[h, 0, rows] = down
            for t in range(BAND):
                dsend[h, t, rows] = (near[t] * down.astype(F32)).astype(BF16)

        return jnp.concatenate(gated, axis=1)

    def norm_part(r):
        landed(mr.at[:, :, rows_of(r)], m_rs.at[r])
        gated = [norm(pl.ds(r * PART + i * step_rows, step_rows)) for i in range(PART // step_rows)]
        gtb[r] = jnp.concatenate(gated, axis=0).T
        g_copy(r).start()
        for h in heads:
            for t in far:
                d_copy(t, h, r).start()
        spread(gtb, r, r)

    def g_copy(r):
        return send(gtb.at[r], gtr.at[r], g_ss.at[0], g_rs.at[r], sib, y)

    def spread(part, r, at):
        gt[:, :, :, at * PART:(at + 1) * PART] = part[r].astype(F32).reshape(NZ, NX, 8, PART)

    def other_part(r):
        landed(gtr.at[r], g_rs.at[r])
        spread(gtr, r, PARTS + r)

    def backward(d, slope, h, q_t, attn_t):
        ds = (dot(d, vt[h]) * slope).astype(BF16)
        return dot(ds, kb[:, cols(h)]), dot(q_t, ds), dot(attn_t, d)

    def own_backward(r):
        lanes = slice(r * PART, (r + 1) * PART)
        for h in heads:
            dq, dk, dv = backward(d3[h, 0, rows_of(r)], slope_own[h, rows_of(r)], h, qt_own[h, :, lanes], attn_own[h, :, lanes])
            dqa[h, rows_of(r)] = dq
            dka[h] = dk if r == 0 else dka[h] + dk
            dva[h] = dv if r == 0 else dva[h] + dv

    def far_backward(h, r):
        landed(d3.at[h, both, rows_of(r)], d_rs.at[h, r])
        dq, dk, dv = backward(flat(d3[h, both, rows_of(r)]), slope_far[h, r], h, qt_far[h, r], attn_far[h, r])
        es[h, :, rows_of(r)] = dq.astype(BF16).reshape(BAND, PART, HEAD_DIM)
        for t in far:
            e_copy(t, h, r).start()
        if r < PARTS - 1:
            dka[h] = dka[h] + dk
            dva[h] = dva[h] + dv
        else:
            dko[:, cols(h)] = (dka[h] + dk).T.astype(BF16)
            dvo[:, cols(h)] = (dva[h] + dv).astype(BF16)

    for h in heads:
        far_forward(h, 0)
    far_forward(0, 1)
    far_forward(1, 1)
    norm_part(0)
    far_forward(2, 1)
    far_forward(3, 1)
    own_backward(0)
    landed(ogs, o_rs.at[0])
    other_part(0)
    norm_part(1)

    piece = NZ * 8
    cut = piece // 2
    low = slice(0, cut)
    high = slice(cut, piece)
    up = at_y(1)
    down = at_y(NY - 1)
    across = at_y(2)

    def ya_copy(k, i):
        return send(ya.at[k, i], yar.at[k, i], ya_ss.at[0], ya_rs.at[k], s, (up, down)[i])

    def yb_copy(k, i):
        return send(yb.at[k, i], ybr.at[k, i], yb_ss.at[0], yb_rs.at[k], s, (up, down)[i])

    def x_copy(k):
        return send(xs.at[k], xr.at[k], x_ss.at[0], x_rs.at[0], at_x(k), y)

    order = (2, 1, 3, 0)
    near_rows = (2 * PARTS - 1) * PART

    def product(k, events, grad):
        return dot(gt[:, x_of(k), :, events].reshape(piece, -1).astype(BF16), grad)

    mine = jnp.concatenate([ogb[core], ogs[:ROWS - PART]], axis=0)
    for k in order:
        part = product(k, slice(0, near_rows), mine)
        for i in range(NY):
            gown[k, i] = part[:, cols(i)]
    far_backward(0, 0)
    other_part(PARTS - 1)

    for k in order:
        part = product(k, slice(near_rows, 2 * ROWS), ogs[ROWS - PART:])
        for i in range(NY):
            gown[k, i] = gown[k, i] + part[:, cols(i)]
        ya[k, 0] = gown[k, across, low].astype(BF16)
        ya[k, 1] = gown[k, across, high].astype(BF16)
        for i in range(2):
            ya_copy(k, i).start()

    def y_pass(k):
        landed(yar.at[k], ya_rs.at[k])
        yb[k, 0, low] = (gown[k, up, low] + yar[k, 0].astype(F32)).astype(BF16)
        yb[k, 0, high] = gown[k, up, high].astype(BF16)
        yb[k, 1, low] = gown[k, down, low].astype(BF16)
        yb[k, 1, high] = (gown[k, down, high] + yar[k, 1].astype(F32)).astype(BF16)
        for i in range(2):
            yb_copy(k, i).start()

    gate_out = pltpu.make_async_copy(dgo, dg_out.at[0], out_sem.at[0])
    gate_out.start()

    def y_sum(k):
        landed(ybr.at[k], yb_rs.at[k])
        return gown[k, y] + ybr[k, 0].astype(F32) + ybr[k, 1].astype(F32)

    def x_start(k):
        xs[k] = y_sum(k).astype(BF16)
        x_copy(k).start()

    far_backward(1, 0)
    far_backward(2, 0)
    far_backward(3, 0)
    for k in order:
        y_pass(k)
    own_backward(1)
    far_backward(0, 1)
    far_backward(1, 1)
    for k in order[:-1]:
        x_start(k)

    z_order = (8, 7, 9, 6, 10, 5, 11, 4, 12, 3, 13, 2, 14, 1, 15)

    def z_copy(m):
        return send(zs.at[lax.rem(z + m, NZ)], zr.at[m], z_ss.at[0], z_rs.at[0], at_z(m), y)

    plane = y_sum(0)
    landed(xr.at[pl.ds(1, NX - 1)], x_rs.at[0])
    for k in range(1, NX):
        plane = plane + xr[k].astype(F32)
    zs[...] = plane.reshape(NZ, 8, 128)
    for m in z_order:
        z_copy(m).start()

    far_backward(2, 1)
    far_backward(3, 1)
    key_out = pltpu.make_async_copy(dko, dk_out.at[0], out_sem.at[1])
    value_out = pltpu.make_async_copy(dvo, dv_out.at[0], out_sem.at[2])
    key_out.start()
    value_out.start()

    def t_copy(dy, dc):
        slot = core * NY + y
        seq = s if dc == 0 else sib
        return send(tiles.at[slot], tiles.at[slot], t_ss.at[0], t_rs.at[0], seq, at_y(dy))

    others = [(dy, dc) for dy in range(NY) for dc in range(2) if (dy, dc) != (0, 0)]

    landed(zr.at[pl.ds(1, NZ - 1)], z_rs.at[0])
    tile = zs[z]
    for m in range(1, NZ):
        tile = tile + zr[m]
    tiles[core * NY + y] = tile
    for dy, dc in others:
        t_copy(dy, dc).start()

    landed(er, e_rs.at[0])
    for h in heads:
        dqo[:, cols(h)] = (dqa[h] + er[h, 0].astype(F32) + er[h, 1].astype(F32)).astype(BF16)
    query_out = pltpu.make_async_copy(dqo, dq_out.at[0], out_sem.at[3])
    query_out.start()

    for ref, sem in (
        (ps, q_ss), (ps, m_ss), (dsend, d_ss), (es, e_ss), (ogs, o_ss), (gtb, g_ss), (ya, ya_ss), (yb, yb_ss),
        (xs.at[pl.ds(1, NX - 1)], x_ss), (zs.at[pl.ds(0, NZ - 1)], z_ss),
    ):
        sent(ref, sem.at[0])
    for out in (gate_out, key_out, value_out, query_out):
        out.wait()

    arrived = tiles.at[pl.ds(0, 2 * NY - 1)]
    landed(arrived, t_rs.at[0])
    lower = jnp.broadcast_to(core, (4, 128)) == 0
    for slot in range(2 * NY):
        full = tiles[slot]
        wg_out[:, slot * 128:(slot + 1) * 128] = jnp.where(lower, full[:4], full[4:])
    sent(arrived, t_ss.at[0])


def finish(*refs):
    sem = refs[-1]
    n = len(refs) // 2
    copies = [pltpu.make_async_copy(refs[i], refs[n + i], sem.at[i]) for i in range(n)]
    for copy in copies:
        copy.start()
    for copy in copies:
        copy.wait()


def finished(arrays):
    anywhere = pl.BlockSpec(memory_space=pl.ANY)
    return pl.pallas_call(
        finish,
        out_shape=tuple(jax.ShapeDtypeStruct(a.shape, a.dtype) for a in arrays),
        in_specs=[pl.BlockSpec(memory_space=pltpu.VMEM)] * len(arrays),
        out_specs=(anywhere,) * len(arrays),
        scratch_shapes=[pltpu.SemaphoreType.DMA((len(arrays),))],
        compiler_params=pltpu.CompilerParams(vmem_limit_bytes=16 * 1024 * 1024),
    )(*arrays)


def local(queries, keys, values, gates, out_weight, out_grad, lengths, pattern):
    block = (HEADS, ROWS, HEAD_DIM)
    block_t = (HEADS, HEAD_DIM, ROWS)
    two = (HEADS, BAND, ROWS, HEAD_DIM)
    three = (HEADS, BAND + 1, ROWS, HEAD_DIM)
    band = (BAND + 1, ROWS, ROWS)
    rows = (ROWS, WIDTH)
    vmem = pltpu.VMEM
    smem = pltpu.SMEM
    scratch = [
        smem(lengths.shape, jnp.int32), smem(pattern.shape, jnp.int32),
        vmem(three, BF16), vmem(rows, BF16), vmem(rows, BF16), vmem(rows, BF16),
        vmem((2,) + rows, BF16), vmem(rows, BF16), vmem((WIDTH, MODEL), BF16),
        vmem(block_t, BF16), vmem(block_t, BF16),
        vmem(band, F32), vmem(band, F32), vmem(block, F32), vmem(block, F32),
        vmem(two, BF16), vmem(two, BF16),
        vmem(three, BF16), vmem(two, BF16), vmem(two, BF16), vmem(two, BF16),
        vmem((HEADS, ROWS, ROWS), BF16), vmem((HEADS, PARTS, ROWS, BAND * PART), BF16),
        vmem(block_t, BF16), vmem((HEADS, PARTS, HEAD_DIM, BAND * PART), BF16),
        vmem((HEADS, ROWS, ROWS), F32), vmem((HEADS, PARTS, BAND * PART, ROWS), F32),
        vmem((NZ, NX, 8, 2 * ROWS), F32), vmem((PARTS, WIDTH, PART), BF16), vmem((PARTS, WIDTH, PART), BF16),
        vmem((NX, NY, NZ * 8, 128), F32),
        vmem((NX, 2, NZ * 4, 128), BF16), vmem((NX, 2, NZ * 4, 128), BF16),
        vmem((NX, 2, NZ * 8, 128), BF16), vmem((NX, 2, NZ * 8, 128), BF16),
        vmem((NX, NZ * 8, 128), BF16), vmem((NX, NZ * 8, 128), BF16),
        vmem((NZ, 8, 128), F32), vmem((NZ, 8, 128), F32), vmem((2 * NY, 8, 128), F32),
        vmem(block, F32), vmem(block_t, F32), vmem(block, F32),
        vmem(rows, BF16), vmem(rows, BF16), vmem(rows, BF16), vmem(rows, BF16),
    ]
    dma = pltpu.SemaphoreType.DMA
    one = dma((1,))
    scratch += [dma((13,)), dma((4,))]
    scratch += [one, dma((HEADS, PARTS)), one, dma((PARTS,)), one, dma((HEADS, PARTS)), one, one]
    scratch += [one, one, one, dma((PARTS,)), one, dma((NX,)), one, dma((NX,))]
    scratch += [one] * 6
    anywhere = pl.BlockSpec(memory_space=pl.ANY)
    grad = jax.ShapeDtypeStruct((1, ROWS, WIDTH), BF16)
    operands = (lengths, pattern, queries, keys, values, gates, out_weight, out_grad)
    results = pl.pallas_call(
        kernel,
        out_shape=(grad, grad, grad, grad, jax.ShapeDtypeStruct((WIDTH // N_SEQ, MODEL), F32)),
        in_specs=[anywhere] * len(operands),
        out_specs=(anywhere,) * 4 + (pl.BlockSpec(memory_space=pltpu.VMEM),),
        scratch_shapes=scratch,
        compiler_params=pltpu.CompilerParams(
            collective_id=0, has_side_effects=True, vmem_limit_bytes=40 * 1024 * 1024
        ),
        cost_estimate=pl.CostEstimate(flops=2 * 10**9, bytes_accessed=5 * 2**20, transcendentals=3 * 4 * ROWS * ROWS),
    )(*[pltpu.with_memory_space_constraint(a, pltpu.HBM) for a in operands])
    return finished(results)


def solution(mesh):
    events = P("dp", "seq", None)
    return jax.shard_map(
        local,
        mesh=mesh,
        in_specs=(events, events, events, events, P(), events, P("dp", None), events),
        out_specs=(events, events, events, events, P("seq", None)),
        check_vma=False,
    )
```

```python
import jax
import jax.numpy as jnp
from jax import lax
from jax.experimental import pallas as pl
from jax.experimental.pallas import tpu as pltpu
from jax.sharding import PartitionSpec as P

MESH = pl.DeviceIdType.MESH
EPS = 1e-05
HEADS = 4
HEAD_DIM = 128
ROWS = 256
WIDTH = 512
MODEL = 1024
NX = 4
NZ = 16
NY = 4
N_SEQ = 128
BAND = 2
PARTS = 2
PART = ROWS // PARTS
SCALE = 1.0 / ((BAND + 1) * ROWS)
BF16 = jnp.bfloat16
F32 = jnp.float32
NT = (((1,), (1,)), ((), ()))
TN = (((0,), (0,)), ((), ()))


def dot(a, b):
    return jnp.dot(a, b, preferred_element_type=F32)


def dot_nt(a, b):
    return lax.dot_general(a, b, NT, preferred_element_type=F32)


def dot_tn(a, b):
    return lax.dot_general(a, b, TN, preferred_element_type=F32)


def loop(n, body):
    lax.fori_loop(0, n, lambda i, c: (body(i), c)[1], jnp.int32(0))


def kernel(
    len_in, pat_in, q_in, k_in, v_in, gate_in, w_in, og_in,
    dq_out, dk_out, dv_out, dg_out, wg_out,
    len_ref, pat_ref, q3, kb, vb, gb, ogb, ogs, wb, kt, vt, mask, half, dgt, mix,
    ps, mr, d3, dsend, es, er, attn_own, attn_far, qt_own, qt_far, slope_own, slope_far, gt, gtb, gtr,
    gown, ya, yar, yb, ybr, xs, xr, zs, zr, tiles,
    dqa, dka, dva, dqo, dko, dvo, dgo,
    ld_sem, out_sem, q_ss, q_rs, m_ss, m_rs, d_ss, d_rs, e_ss, e_rs,
    o_ss, o_rs, g_ss, g_rs, ya_ss, ya_rs, yb_ss, yb_rs, x_ss, x_rs, z_ss, z_rs, t_ss, t_rs,
):
    s = lax.axis_index("seq")
    y = lax.axis_index("dp")
    core = lax.rem(s, 2)
    x = lax.rem(s // 2, NX)
    z = s // (2 * NX)
    sib = s + 1 - 2 * core
    heads = range(HEADS)
    far = (2, 1)

    def ring(by):
        return lax.rem(s + by + N_SEQ, N_SEQ)

    def x_of(k):
        return lax.rem(x + k, NX)

    def at_x(k):
        return z * (2 * NX) + x_of(k) * 2 + core

    def at_z(m):
        return lax.rem(z + m, NZ) * (2 * NX) + x * 2 + core

    def at_y(j):
        return lax.rem(y + j, NY)

    barrier = pltpu.get_barrier_semaphore()

    def greet(seq, dp):
        pl.semaphore_signal(barrier, inc=1, device_id={"seq": seq, "dp": dp}, device_id_type=MESH)

    def cols(h):
        return slice(h * HEAD_DIM, (h + 1) * HEAD_DIM)

    for by in (-2, -1, 1, 2):
        greet(ring(by), y)
    q_loads = [pltpu.make_async_copy(q_in.at[0, :, cols(h)], q3.at[h, 0], ld_sem.at[h]) for h in heads]
    for load in q_loads:
        load.start()
    for j in range(1, NY):
        greet(s, at_y(j))
        greet(sib, at_y(j))
    for k in range(1, NX):
        greet(at_x(k), y)
    for m in range(1, NZ):
        greet(at_z(m), y)

    k_load = pltpu.make_async_copy(k_in.at[0], kb, ld_sem.at[4])
    v_load = pltpu.make_async_copy(v_in.at[0], vb, ld_sem.at[5])
    gate_load = pltpu.make_async_copy(gate_in.at[0], gb, ld_sem.at[6])
    og_loads = [pltpu.make_async_copy(og_in.at[0, :, c * WIDTH:(c + 1) * WIDTH], ogb.at[c], ld_sem.at[11 + c]) for c in range(2)]
    w_load = pltpu.make_async_copy(w_in, wb, ld_sem.at[8])
    few_loads = [pltpu.make_async_copy(len_in, len_ref, ld_sem.at[9]), pltpu.make_async_copy(pat_in, pat_ref, ld_sem.at[10])]
    for load in [k_load, v_load] + few_loads + og_loads + [w_load, gate_load]:
        load.start()

    def send(src, dst, ss, rs, seq, dp):
        return pltpu.make_async_remote_copy(
            src_ref=src, dst_ref=dst, send_sem=ss, recv_sem=rs,
            device_id={"seq": seq, "dp": dp}, device_id_type=MESH,
        )

    def rows_of(r):
        return pl.ds(r * PART, PART)

    def band_copy(src, dst, ss, rs, h, r, by):
        return send(src.at[rows_of(r)], dst.at[rows_of(r)], ss.at[0], rs, ring(by), y)

    def q_copy(t, h, r):
        return band_copy(q3.at[h, 0], q3.at[h, t], q_ss, q_rs.at[h, r], h, r, -t)

    def m_copy(t, h, r):
        return band_copy(ps.at[h, t - 1], mr.at[h, t - 1], m_ss, m_rs.at[r], h, r, t)

    def d_copy(t, h, r):
        return band_copy(dsend.at[h, t - 1], d3.at[h, t], d_ss, d_rs.at[h, r], h, r, -t)

    def e_copy(t, h, r):
        return band_copy(es.at[h, t - 1], er.at[h, t - 1], e_ss, e_rs.at[0], h, r, t)

    def landed(ref, sem):
        send(ref, ref, sem, sem, sib, y).wait_recv()

    def sent(ref, sem):
        send(ref, ref, sem, sem, sib, y).wait_send()

    q_loads[0].wait()
    pl.semaphore_wait(barrier, 4 + 2 * (NY - 1) + (NX - 1) + (NZ - 1))
    for r in range(PARTS):
        for h in heads:
            if h and not r:
                q_loads[h].wait()
            for t in far:
                q_copy(t, h, r).start()

    for load in few_loads:
        load.wait()
    ends = []
    total = jnp.int32(0)
    for i in range(len_ref.shape[1]):
        total = total + len_ref[0, i]
        ends.append(total)

    def doc(at):
        number = jnp.zeros(at.shape, jnp.int32)
        for end in ends:
            number = number + jnp.where(at >= end, 1, 0)
        return number

    key_at = s * ROWS + lax.broadcasted_iota(jnp.int32, (1, ROWS), 1)
    key_doc = doc(key_at)
    for t in range(BAND + 1):
        query_at = (s + t) * ROWS + lax.broadcasted_iota(jnp.int32, (ROWS, 1), 0)
        keep = (doc(query_at) == key_doc) & (key_at <= query_at)
        mask[t] = jnp.where(keep, SCALE, 0.0).astype(F32)
        half[t] = jnp.where(keep, 0.5 * SCALE, 0.0).astype(F32)

    own = slice(0, 1)
    both = pl.ds(1, BAND)

    def flat(array):
        return array.reshape(-1, array.shape[-1])

    def forward(ts, rows, h):
        q = flat(q3[h, ts, rows])
        scores = dot(q, kt[h])
        middle = 0.5 * scores
        tanh = jnp.tanh(middle)
        twice = 1.0 + tanh
        silu = middle * twice
        a = (silu * flat(mask[ts, rows])).astype(BF16)
        slope = (twice + silu * (1.0 - tanh)) * flat(half[ts, rows])
        return q, a, slope, dot(a, vb[:, cols(h)])

    k_load.wait()
    for h in heads:
        kt[h] = kb[:, cols(h)].T
    v_load.wait()
    for h in heads:
        vt[h] = vb[:, cols(h)].T
    made = [forward(own, pl.ds(0, ROWS), h) for h in heads]
    for h, (q, a, slope, part) in zip(heads, made):
        slope_own[h] = slope
        mix[h] = part
        attn_own[h] = a.T
        qt_own[h] = q.T

    for load in og_loads:
        load.wait()
    swap = send(ogb.at[1 - core], ogs, o_ss.at[0], o_rs.at[0], sib, y)
    swap.start()
    w_load.wait()
    og = jnp.concatenate([ogb[0], ogb[1]], axis=1)
    for i in range(2):
        part = dot_nt(og, wb[pl.ds(i * 256, 256), :])
        dgt[2 * i] = part[:, :HEAD_DIM]
        dgt[2 * i + 1] = part[:, HEAD_DIM:]
    gate_load.wait()

    def far_forward(group, r):
        for h in group:
            landed(q3.at[h, both, rows_of(r)], q_rs.at[h, r])
        made = [forward(both, rows_of(r), h) for h in group]
        for h, (_, _, slope, part) in zip(group, made):
            ps[h, :, rows_of(r)] = part.astype(BF16).reshape(BAND, PART, HEAD_DIM)
            slope_far[h, r] = slope
        for h in group:
            for t in far:
                m_copy(t, h, r).start()
        for h, (q, a, _, _) in zip(group, made):
            attn_far[h, r] = a.T
            qt_far[h, r] = q.T

    near = [jnp.where(pat_ref[0, 0, t] > 0, 1.0, 0.0).astype(F32) for t in range(BAND)]

    step_rows = 64

    def norm(rows):
        def mean(parts):
            return jnp.sum(sum(parts[1:], parts[0]), axis=1, keepdims=True) * (1.0 / WIDTH)

        mixed = [
            mix[h, rows] + near[0] * mr[h, 0, rows].astype(F32) + near[1] * mr[h, 1, rows].astype(F32) for h in heads
        ]
        centre = mean(mixed)
        mixed = [m - centre for m in mixed]
        inv = lax.rsqrt(mean([m * m for m in mixed]) + EPS)
        normed = [m * inv for m in mixed]
        grad = []
        gated = []
        for h in heads:
            gate = gb[rows, cols(h)].astype(F32)
            gated.append((normed[h] * gate).astype(BF16))
            up = dgt[h, rows]
            dgo[rows, cols(h)] = (up * normed[h]).astype(BF16)
            grad.append(up * gate)
        first = mean(grad)
        second = mean([g * n for g, n in zip(grad, normed)])
        for h in heads:
            down = (inv * (grad[h] - first - normed[h] * second)).astype(BF16)
            d3[h, 0, rows] = down
            for t in range(BAND):
                dsend[h, t, rows] = (near[t] * down.astype(F32)).astype(BF16)

        return jnp.concatenate(gated, axis=1)

    def norm_part(r):
        landed(mr.at[:, :, rows_of(r)], m_rs.at[r])
        gated = [norm(pl.ds(r * PART + i * step_rows, step_rows)) for i in range(PART // step_rows)]
        gtb[r] = jnp.concatenate(gated, axis=0).T
        g_copy(r).start()
        for h in heads:
            for t in far:
                d_copy(t, h, r).start()
        spread(gtb, r, r)

    def g_copy(r):
        return send(gtb.at[r], gtr.at[r], g_ss.at[0], g_rs.at[r], sib, y)

    def spread(part, r, at):
        gt[:, :, :, at * PART:(at + 1) * PART] = part[r].astype(F32).reshape(NZ, NX, 8, PART)

    def other_part(r):
        landed(gtr.at[r], g_rs.at[r])
        spread(gtr, r, PARTS + r)

    def backward(d, slope, h, q_t, attn_t):
        ds = (dot(d, vt[h]) * slope).astype(BF16)
        return dot(ds, kb[:, cols(h)]), dot(q_t, ds), dot(attn_t, d)

    def own_backward(r):
        lanes = slice(r * PART, (r + 1) * PART)
        made = [
            backward(d3[h, 0, rows_of(r)], slope_own[h, rows_of(r)], h, qt_own[h, :, lanes], attn_own[h, :, lanes]) for h in heads
        ]
        for h, (dq, dk, dv) in zip(heads, made):
            dqa[h, rows_of(r)] = dq
            dka[h] = dk if r == 0 else dka[h] + dk
            dva[h] = dv if r == 0 else dva[h] + dv

    def far_backward(group, r):
        for h in group:
            landed(d3.at[h, both, rows_of(r)], d_rs.at[h, r])
        made = [
            backward(flat(d3[h, both, rows_of(r)]), slope_far[h, r], h, qt_far[h, r], attn_far[h, r]) for h in group
        ]
        for h, (dq, dk, dv) in zip(group, made):
            es[h, :, rows_of(r)] = dq.astype(BF16).reshape(BAND, PART, HEAD_DIM)
            if r < PARTS - 1:
                dka[h] = dka[h] + dk
                dva[h] = dva[h] + dv
            else:
                dko[:, cols(h)] = (dka[h] + dk).T.astype(BF16)
                dvo[:, cols(h)] = (dva[h] + dv).astype(BF16)
        for h in group:
            for t in far:
                e_copy(t, h, r).start()

    first, last = (0, 1), (2, 3)
    far_forward(first, 0)
    far_forward(last, 0)
    far_forward(first, 1)
    norm_part(0)
    far_forward((2,), 1)
    far_forward((3,), 1)
    own_backward(0)
    landed(ogs, o_rs.at[0])
    other_part(0)
    norm_part(1)

    piece = NZ * 8
    cut = piece // 2
    low = slice(0, cut)
    high = slice(cut, piece)
    up = at_y(1)
    down = at_y(NY - 1)
    across = at_y(2)

    def ya_copy(k, i):
        return send(ya.at[k, i], yar.at[k, i], ya_ss.at[0], ya_rs.at[k], s, (up, down)[i])

    def yb_copy(k, i):
        return send(yb.at[k, i], ybr.at[k, i], yb_ss.at[0], yb_rs.at[k], s, (up, down)[i])

    def x_copy(k):
        return send(xs.at[k], xr.at[k], x_ss.at[0], x_rs.at[0], at_x(k), y)

    order = (2, 1, 3, 0)
    near_rows = (2 * PARTS - 1) * PART

    def product(k, events, grad):
        return dot(gt[:, x_of(k), :, events].reshape(piece, -1).astype(BF16), grad)

    mine = jnp.concatenate([ogb[core], ogs[:ROWS - PART]], axis=0)
    for k in order:
        part = product(k, slice(0, near_rows), mine)
        for i in range(NY):
            gown[k, i] = part[:, cols(i)]
    far_backward(first, 0)
    other_part(PARTS - 1)

    for k in order:
        part = product(k, slice(near_rows, 2 * ROWS), ogs[ROWS - PART:])
        for i in range(NY):
            gown[k, i] = gown[k, i] + part[:, cols(i)]
        ya[k, 0] = gown[k, across, low].astype(BF16)
        ya[k, 1] = gown[k, across, high].astype(BF16)
        for i in range(2):
            ya_copy(k, i).start()

    def y_pass(k):
        landed(yar.at[k], ya_rs.at[k])
        yb[k, 0, low] = (gown[k, up, low] + yar[k, 0].astype(F32)).astype(BF16)
        yb[k, 0, high] = gown[k, up, high].astype(BF16)
        yb[k, 1, low] = gown[k, down, low].astype(BF16)
        yb[k, 1, high] = (gown[k, down, high] + yar[k, 1].astype(F32)).astype(BF16)
        for i in range(2):
            yb_copy(k, i).start()

    gate_out = pltpu.make_async_copy(dgo, dg_out.at[0], out_sem.at[0])
    gate_out.start()

    def y_sum(k):
        landed(ybr.at[k], yb_rs.at[k])
        return gown[k, y] + ybr[k, 0].astype(F32) + ybr[k, 1].astype(F32)

    def x_start(k):
        xs[k] = y_sum(k).astype(BF16)
        x_copy(k).start()

    far_backward(last, 0)
    for k in order:
        y_pass(k)
    own_backward(1)
    far_backward(first, 1)
    for k in order[:-1]:
        x_start(k)

    z_order = (8, 7, 9, 6, 10, 5, 11, 4, 12, 3, 13, 2, 14, 1, 15)

    def z_copy(m):
        return send(zs.at[lax.rem(z + m, NZ)], zr.at[m], z_ss.at[0], z_rs.at[0], at_z(m), y)

    plane = y_sum(0)
    landed(xr.at[pl.ds(1, NX - 1)], x_rs.at[0])
    for k in range(1, NX):
        plane = plane + xr[k].astype(F32)
    zs[...] = plane.reshape(NZ, 8, 128)
    for m in z_order:
        z_copy(m).start()

    far_backward(last, 1)
    key_out = pltpu.make_async_copy(dko, dk_out.at[0], out_sem.at[1])
    value_out = pltpu.make_async_copy(dvo, dv_out.at[0], out_sem.at[2])
    key_out.start()
    value_out.start()

    def t_copy(dy, dc):
        slot = core * NY + y
        seq = s if dc == 0 else sib
        return send(tiles.at[slot], tiles.at[slot], t_ss.at[0], t_rs.at[0], seq, at_y(dy))

    others = [(dy, dc) for dy in range(NY) for dc in range(2) if (dy, dc) != (0, 0)]

    landed(zr.at[pl.ds(1, NZ - 1)], z_rs.at[0])
    tile = zs[z]
    for m in range(1, NZ):
        tile = tile + zr[m]
    tiles[core * NY + y] = tile
    for dy, dc in others:
        t_copy(dy, dc).start()

    landed(er, e_rs.at[0])
    for h in heads:
        dqo[:, cols(h)] = (dqa[h] + er[h, 0].astype(F32) + er[h, 1].astype(F32)).astype(BF16)
    query_out = pltpu.make_async_copy(dqo, dq_out.at[0], out_sem.at[3])
    query_out.start()

    for ref, sem in (
        (ps, q_ss), (ps, m_ss), (dsend, d_ss), (es, e_ss), (ogs, o_ss), (gtb, g_ss), (ya, ya_ss), (yb, yb_ss),
        (xs.at[pl.ds(1, NX - 1)], x_ss), (zs.at[pl.ds(0, NZ - 1)], z_ss),
    ):
        sent(ref, sem.at[0])
    for out in (gate_out, key_out, value_out, query_out):
        out.wait()

    arrived = tiles.at[pl.ds(0, 2 * NY - 1)]
    landed(arrived, t_rs.at[0])
    lower = jnp.broadcast_to(core, (4, 128)) == 0
    for slot in range(2 * NY):
        full = tiles[slot]
        wg_out[:, slot * 128:(slot + 1) * 128] = jnp.where(lower, full[:4], full[4:])
    sent(arrived, t_ss.at[0])


def finish(*refs):
    sem = refs[-1]
    n = len(refs) // 2
    copies = [pltpu.make_async_copy(refs[i], refs[n + i], sem.at[i]) for i in range(n)]
    for copy in copies:
        copy.start()
    for copy in copies:
        copy.wait()


def finished(arrays):
    anywhere = pl.BlockSpec(memory_space=pl.ANY)
    return pl.pallas_call(
        finish,
        out_shape=tuple(jax.ShapeDtypeStruct(a.shape, a.dtype) for a in arrays),
        in_specs=[pl.BlockSpec(memory_space=pltpu.VMEM)] * len(arrays),
        out_specs=(anywhere,) * len(arrays),
        scratch_shapes=[pltpu.SemaphoreType.DMA((len(arrays),))],
        compiler_params=pltpu.CompilerParams(vmem_limit_bytes=16 * 1024 * 1024),
    )(*arrays)


def local(queries, keys, values, gates, out_weight, out_grad, lengths, pattern):
    block = (HEADS, ROWS, HEAD_DIM)
    block_t = (HEADS, HEAD_DIM, ROWS)
    two = (HEADS, BAND, ROWS, HEAD_DIM)
    three = (HEADS, BAND + 1, ROWS, HEAD_DIM)
    band = (BAND + 1, ROWS, ROWS)
    rows = (ROWS, WIDTH)
    vmem = pltpu.VMEM
    smem = pltpu.SMEM
    scratch = [
        smem(lengths.shape, jnp.int32), smem(pattern.shape, jnp.int32),
        vmem(three, BF16), vmem(rows, BF16), vmem(rows, BF16), vmem(rows, BF16),
        vmem((2,) + rows, BF16), vmem(rows, BF16), vmem((WIDTH, MODEL), BF16),
        vmem(block_t, BF16), vmem(block_t, BF16),
        vmem(band, F32), vmem(band, F32), vmem(block, F32), vmem(block, F32),
        vmem(two, BF16), vmem(two, BF16),
        vmem(three, BF16), vmem(two, BF16), vmem(two, BF16), vmem(two, BF16),
        vmem((HEADS, ROWS, ROWS), BF16), vmem((HEADS, PARTS, ROWS, BAND * PART), BF16),
        vmem(block_t, BF16), vmem((HEADS, PARTS, HEAD_DIM, BAND * PART), BF16),
        vmem((HEADS, ROWS, ROWS), F32), vmem((HEADS, PARTS, BAND * PART, ROWS), F32),
        vmem((NZ, NX, 8, 2 * ROWS), F32), vmem((PARTS, WIDTH, PART), BF16), vmem((PARTS, WIDTH, PART), BF16),
        vmem((NX, NY, NZ * 8, 128), F32),
        vmem((NX, 2, NZ * 4, 128), BF16), vmem((NX, 2, NZ * 4, 128), BF16),
        vmem((NX, 2, NZ * 8, 128), BF16), vmem((NX, 2, NZ * 8, 128), BF16),
        vmem((NX, NZ * 8, 128), BF16), vmem((NX, NZ * 8, 128), BF16),
        vmem((NZ, 8, 128), F32), vmem((NZ, 8, 128), F32), vmem((2 * NY, 8, 128), F32),
        vmem(block, F32), vmem(block_t, F32), vmem(block, F32),
        vmem(rows, BF16), vmem(rows, BF16), vmem(rows, BF16), vmem(rows, BF16),
    ]
    dma = pltpu.SemaphoreType.DMA
    one = dma((1,))
    scratch += [dma((13,)), dma((4,))]
    scratch += [one, dma((HEADS, PARTS)), one, dma((PARTS,)), one, dma((HEADS, PARTS)), one, one]
    scratch += [one, one, one, dma((PARTS,)), one, dma((NX,)), one, dma((NX,))]
    scratch += [one] * 6
    anywhere = pl.BlockSpec(memory_space=pl.ANY)
    grad = jax.ShapeDtypeStruct((1, ROWS, WIDTH), BF16)
    operands = (lengths, pattern, queries, keys, values, gates, out_weight, out_grad)
    results = pl.pallas_call(
        kernel,
        out_shape=(grad, grad, grad, grad, jax.ShapeDtypeStruct((WIDTH // N_SEQ, MODEL), F32)),
        in_specs=[anywhere] * len(operands),
        out_specs=(anywhere,) * 4 + (pl.BlockSpec(memory_space=pltpu.VMEM),),
        scratch_shapes=scratch,
        compiler_params=pltpu.CompilerParams(
            collective_id=0, has_side_effects=True, vmem_limit_bytes=40 * 1024 * 1024
        ),
        cost_estimate=pl.CostEstimate(flops=2 * 10**9, bytes_accessed=5 * 2**20, transcendentals=3 * 4 * ROWS * ROWS),
    )(*[pltpu.with_memory_space_constraint(a, pltpu.HBM) for a in operands])
    return finished(results)


def solution(mesh):
    events = P("dp", "seq", None)
    return jax.shard_map(
        local,
        mesh=mesh,
        in_specs=(events, events, events, events, P(), events, P("dp", None), events),
        out_specs=(events, events, events, events, P("seq", None)),
        check_vma=False,
    )
```

```python
import jax
import jax.numpy as jnp
from jax import lax
from jax.experimental import pallas as pl
from jax.experimental.pallas import tpu as pltpu
from jax.sharding import PartitionSpec as P

MESH = pl.DeviceIdType.MESH
EPS = 1e-05
HEADS = 4
HEAD_DIM = 128
ROWS = 256
WIDTH = 512
MODEL = 1024
NX = 4
NZ = 16
NY = 4
N_SEQ = 128
BAND = 2
PARTS = 2
PART = ROWS // PARTS
SCALE = 1.0 / ((BAND + 1) * ROWS)
BF16 = jnp.bfloat16
F32 = jnp.float32
NT = (((1,), (1,)), ((), ()))
TN = (((0,), (0,)), ((), ()))


def dot(a, b):
    return jnp.dot(a, b, preferred_element_type=F32)


def dot_nt(a, b):
    return lax.dot_general(a, b, NT, preferred_element_type=F32)


def dot_tn(a, b):
    return lax.dot_general(a, b, TN, preferred_element_type=F32)


def loop(n, body):
    lax.fori_loop(0, n, lambda i, c: (body(i), c)[1], jnp.int32(0))


def kernel(
    len_in, pat_in, q_in, k_in, v_in, gate_in, w_in, og_in,
    dq_out, dk_out, dv_out, dg_out, wg_out,
    len_ref, pat_ref, q3, kb, vb, gb, ogb, ogs, wb, kt, vt, mask, half, dgt, mix,
    ps, mr, d3, dsend, es, er, attn_own, attn_far, qt_own, qt_far, slope_own, slope_far, gt, gtb, gtr,
    gown, ya, yar, yb, ybr, xs, xr, zs, zr, tiles,
    dqa, dka, dva, dqo, dko, dvo, dgo,
    ld_sem, out_sem, q_ss, q_rs, m_ss, m_rs, d_ss, d_rs, e_ss, e_rs,
    o_ss, o_rs, g_ss, g_rs, ya_ss, ya_rs, yb_ss, yb_rs, x_ss, x_rs, z_ss, z_rs, t_ss, t_rs,
):
    s = lax.axis_index("seq")
    y = lax.axis_index("dp")
    core = lax.rem(s, 2)
    x = lax.rem(s // 2, NX)
    z = s // (2 * NX)
    sib = s + 1 - 2 * core
    heads = range(HEADS)
    far = (2, 1)

    def ring(by):
        return lax.rem(s + by + N_SEQ, N_SEQ)

    def x_of(k):
        return lax.rem(x + k, NX)

    def at_x(k):
        return z * (2 * NX) + x_of(k) * 2 + core

    def at_z(m):
        return lax.rem(z + m, NZ) * (2 * NX) + x * 2 + core

    def at_y(j):
        return lax.rem(y + j, NY)

    barrier = pltpu.get_barrier_semaphore()

    def greet(seq, dp):
        pl.semaphore_signal(barrier, inc=1, device_id={"seq": seq, "dp": dp}, device_id_type=MESH)

    def cols(h):
        return slice(h * HEAD_DIM, (h + 1) * HEAD_DIM)

    for by in (-2, -1, 1, 2):
        greet(ring(by), y)
    q_loads = [pltpu.make_async_copy(q_in.at[0, :, cols(h)], q3.at[h, 0], ld_sem.at[h]) for h in heads]
    for load in q_loads:
        load.start()
    for j in range(1, NY):
        greet(s, at_y(j))
        greet(sib, at_y(j))
    for k in range(1, NX):
        greet(at_x(k), y)
    for m in range(1, NZ):
        greet(at_z(m), y)

    k_load = pltpu.make_async_copy(k_in.at[0], kb, ld_sem.at[4])
    v_load = pltpu.make_async_copy(v_in.at[0], vb, ld_sem.at[5])
    gate_load = pltpu.make_async_copy(gate_in.at[0], gb, ld_sem.at[6])
    og_loads = [pltpu.make_async_copy(og_in.at[0, :, c * WIDTH:(c + 1) * WIDTH], ogb.at[c], ld_sem.at[11 + c]) for c in range(2)]
    w_load = pltpu.make_async_copy(w_in, wb, ld_sem.at[8])
    few_loads = [pltpu.make_async_copy(len_in, len_ref, ld_sem.at[9]), pltpu.make_async_copy(pat_in, pat_ref, ld_sem.at[10])]
    for load in [k_load, v_load] + few_loads + og_loads + [w_load, gate_load]:
        load.start()

    def send(src, dst, ss, rs, seq, dp):
        return pltpu.make_async_remote_copy(
            src_ref=src, dst_ref=dst, send_sem=ss, recv_sem=rs,
            device_id={"seq": seq, "dp": dp}, device_id_type=MESH,
        )

    def rows_of(r):
        return pl.ds(r * PART, PART)

    def band_copy(src, dst, ss, rs, h, r, by):
        return send(src.at[rows_of(r)], dst.at[rows_of(r)], ss.at[0], rs, ring(by), y)

    def q_copy(t, h, r):
        return band_copy(q3.at[h, 0], q3.at[h, t], q_ss, q_rs.at[h, r], h, r, -t)

    def m_copy(t, h, r):
        return band_copy(ps.at[h, t - 1], mr.at[h, t - 1], m_ss, m_rs.at[r], h, r, t)

    def d_copy(t, h, r):
        return band_copy(dsend.at[h, t - 1], d3.at[h, t], d_ss, d_rs.at[h, r], h, r, -t)

    def e_copy(t, h, r):
        return band_copy(es.at[h, t - 1], er.at[h, t - 1], e_ss, e_rs.at[0], h, r, t)

    def landed(ref, sem):
        send(ref, ref, sem, sem, sib, y).wait_recv()

    def sent(ref, sem):
        send(ref, ref, sem, sem, sib, y).wait_send()

    q_loads[0].wait()
    pl.semaphore_wait(barrier, 4 + 2 * (NY - 1) + (NX - 1) + (NZ - 1))
    for r in range(PARTS):
        for h in heads:
            if h and not r:
                q_loads[h].wait()
            for t in far:
                q_copy(t, h, r).start()

    for load in few_loads:
        load.wait()
    ends = []
    total = jnp.int32(0)
    for i in range(len_ref.shape[1]):
        total = total + len_ref[0, i]
        ends.append(total)

    def doc(at):
        number = jnp.zeros(at.shape, jnp.int32)
        for end in ends:
            number = number + jnp.where(at >= end, 1, 0)
        return number

    key_at = s * ROWS + lax.broadcasted_iota(jnp.int32, (1, ROWS), 1)
    key_doc = doc(key_at)
    for t in range(BAND + 1):
        query_at = (s + t) * ROWS + lax.broadcasted_iota(jnp.int32, (ROWS, 1), 0)
        keep = (doc(query_at) == key_doc) & (key_at <= query_at)
        mask[t] = jnp.where(keep, SCALE, 0.0).astype(F32)
        half[t] = jnp.where(keep, 0.5 * SCALE, 0.0).astype(F32)

    own = slice(0, 1)
    both = pl.ds(1, BAND)

    def flat(array):
        return array.reshape(-1, array.shape[-1])

    def forward(ts, rows, h):
        q = flat(q3[h, ts, rows])
        scores = dot(q, kt[h])
        middle = 0.5 * scores
        tanh = jnp.tanh(middle)
        twice = 1.0 + tanh
        silu = middle * twice
        a = (silu * flat(mask[ts, rows])).astype(BF16)
        slope = (twice + silu * (1.0 - tanh)) * flat(half[ts, rows])
        return q, a, slope, dot(a, vb[:, cols(h)])

    k_load.wait()
    for h in heads:
        kt[h] = kb[:, cols(h)].T
    v_load.wait()
    for h in heads:
        vt[h] = vb[:, cols(h)].T
    def own_forward(h):
        q, a, slope_own[h], mix[h] = forward(own, pl.ds(0, ROWS), h)
        attn_own[h] = a.T
        qt_own[h] = q.T

    def up_rows(i):
        og = jnp.concatenate([ogb[0], ogb[1]], axis=1)
        part = dot_nt(og, wb[pl.ds(i * 256, 256), :])
        dgt[2 * i] = part[:, :HEAD_DIM]
        dgt[2 * i + 1] = part[:, HEAD_DIM:]

    own_forward(0)
    for load in og_loads:
        load.wait()
    swap = send(ogb.at[1 - core], ogs, o_ss.at[0], o_rs.at[0], sib, y)
    swap.start()
    own_forward(1)

    def far_forward(h, r):
        landed(q3.at[h, both, rows_of(r)], q_rs.at[h, r])
        q, a, slope_far[h, r], part = forward(both, rows_of(r), h)
        ps[h, :, rows_of(r)] = part.astype(BF16).reshape(BAND, PART, HEAD_DIM)
        for t in far:
            m_copy(t, h, r).start()
        attn_far[h, r] = a.T
        qt_far[h, r] = q.T

    near = [jnp.where(pat_ref[0, 0, t] > 0, 1.0, 0.0).astype(F32) for t in range(BAND)]

    step_rows = 64

    def norm(rows):
        def mean(parts):
            return jnp.sum(sum(parts[1:], parts[0]), axis=1, keepdims=True) * (1.0 / WIDTH)

        mixed = [
            mix[h, rows] + near[0] * mr[h, 0, rows].astype(F32) + near[1] * mr[h, 1, rows].astype(F32) for h in heads
        ]
        centre = mean(mixed)
        mixed = [m - centre for m in mixed]
        inv = lax.rsqrt(mean([m * m for m in mixed]) + EPS)
        normed = [m * inv for m in mixed]
        grad = []
        gated = []
        for h in heads:
            gate = gb[rows, cols(h)].astype(F32)
            gated.append((normed[h] * gate).astype(BF16))
            up = dgt[h, rows]
            dgo[rows, cols(h)] = (up * normed[h]).astype(BF16)
            grad.append(up * gate)
        first = mean(grad)
        second = mean([g * n for g, n in zip(grad, normed)])
        for h in heads:
            down = (inv * (grad[h] - first - normed[h] * second)).astype(BF16)
            d3[h, 0, rows] = down
            for t in range(BAND):
                dsend[h, t, rows] = (near[t] * down.astype(F32)).astype(BF16)

        return jnp.concatenate(gated, axis=1)

    def norm_part(r):
        landed(mr.at[:, :, rows_of(r)], m_rs.at[r])
        gated = [norm(pl.ds(r * PART + i * step_rows, step_rows)) for i in range(PART // step_rows)]
        gtb[r] = jnp.concatenate(gated, axis=0).T
        g_copy(r).start()
        for h in heads:
            for t in far:
                d_copy(t, h, r).start()
        spread(gtb, r, r)

    def g_copy(r):
        return send(gtb.at[r], gtr.at[r], g_ss.at[0], g_rs.at[r], sib, y)

    def spread(part, r, at):
        gt[:, :, :, at * PART:(at + 1) * PART] = part[r].astype(F32).reshape(NZ, NX, 8, PART)

    def other_part(r):
        landed(gtr.at[r], g_rs.at[r])
        spread(gtr, r, PARTS + r)

    def backward(d, slope, h, q_t, attn_t):
        ds = (dot(d, vt[h]) * slope).astype(BF16)
        return dot(ds, kb[:, cols(h)]), dot(q_t, ds), dot(attn_t, d)

    def own_backward(r):
        lanes = slice(r * PART, (r + 1) * PART)
        for h in heads:
            dq, dk, dv = backward(d3[h, 0, rows_of(r)], slope_own[h, rows_of(r)], h, qt_own[h, :, lanes], attn_own[h, :, lanes])
            dqa[h, rows_of(r)] = dq
            dka[h] = dk if r == 0 else dka[h] + dk
            dva[h] = dv if r == 0 else dva[h] + dv

    def far_backward(h, r):
        landed(d3.at[h, both, rows_of(r)], d_rs.at[h, r])
        dq, dk, dv = backward(flat(d3[h, both, rows_of(r)]), slope_far[h, r], h, qt_far[h, r], attn_far[h, r])
        es[h, :, rows_of(r)] = dq.astype(BF16).reshape(BAND, PART, HEAD_DIM)
        for t in far:
            e_copy(t, h, r).start()
        if r < PARTS - 1:
            dka[h] = dka[h] + dk
            dva[h] = dva[h] + dv
        else:
            dko[:, cols(h)] = (dka[h] + dk).T.astype(BF16)
            dvo[:, cols(h)] = (dva[h] + dv).astype(BF16)

    far_forward(0, 0)
    own_forward(2)
    far_forward(1, 0)
    own_forward(3)
    far_forward(2, 0)
    w_load.wait()
    up_rows(0)
    far_forward(3, 0)
    up_rows(1)
    far_forward(0, 1)
    gate_load.wait()
    far_forward(1, 1)
    norm_part(0)
    far_forward(2, 1)
    far_forward(3, 1)
    own_backward(0)
    landed(ogs, o_rs.at[0])
    other_part(0)
    norm_part(1)

    piece = NZ * 8
    cut = piece // 2
    low = slice(0, cut)
    high = slice(cut, piece)
    up = at_y(1)
    down = at_y(NY - 1)
    across = at_y(2)

    def ya_copy(k, i):
        return send(ya.at[k, i], yar.at[k, i], ya_ss.at[0], ya_rs.at[k], s, (up, down)[i])

    def yb_copy(k, i):
        return send(yb.at[k, i], ybr.at[k, i], yb_ss.at[0], yb_rs.at[k], s, (up, down)[i])

    def x_copy(k):
        return send(xs.at[k], xr.at[k], x_ss.at[0], x_rs.at[0], at_x(k), y)

    order = (2, 1, 3, 0)
    near_rows = (2 * PARTS - 1) * PART

    def product(k, events, grad):
        return dot(gt[:, x_of(k), :, events].reshape(piece, -1).astype(BF16), grad)

    mine = jnp.concatenate([ogb[core], ogs[:ROWS - PART]], axis=0)
    for k in order:
        part = product(k, slice(0, near_rows), mine)
        for i in range(NY):
            gown[k, i] = part[:, cols(i)]
    far_backward(0, 0)
    other_part(PARTS - 1)

    for k in order:
        part = product(k, slice(near_rows, 2 * ROWS), ogs[ROWS - PART:])
        for i in range(NY):
            gown[k, i] = gown[k, i] + part[:, cols(i)]
        ya[k, 0] = gown[k, across, low].astype(BF16)
        ya[k, 1] = gown[k, across, high].astype(BF16)
        for i in range(2):
            ya_copy(k, i).start()

    def y_pass(k):
        landed(yar.at[k], ya_rs.at[k])
        yb[k, 0, low] = (gown[k, up, low] + yar[k, 0].astype(F32)).astype(BF16)
        yb[k, 0, high] = gown[k, up, high].astype(BF16)
        yb[k, 1, low] = gown[k, down, low].astype(BF16)
        yb[k, 1, high] = (gown[k, down, high] + yar[k, 1].astype(F32)).astype(BF16)
        for i in range(2):
            yb_copy(k, i).start()

    gate_out = pltpu.make_async_copy(dgo, dg_out.at[0], out_sem.at[0])
    gate_out.start()

    def y_sum(k):
        landed(ybr.at[k], yb_rs.at[k])
        return gown[k, y] + ybr[k, 0].astype(F32) + ybr[k, 1].astype(F32)

    def x_start(k):
        xs[k] = y_sum(k).astype(BF16)
        x_copy(k).start()

    far_backward(1, 0)
    far_backward(2, 0)
    far_backward(3, 0)
    for k in order:
        y_pass(k)
    own_backward(1)
    far_backward(0, 1)
    far_backward(1, 1)
    for k in order[:-1]:
        x_start(k)

    z_order = (8, 7, 9, 6, 10, 5, 11, 4, 12, 3, 13, 2, 14, 1, 15)

    def z_copy(m):
        return send(zs.at[lax.rem(z + m, NZ)], zr.at[m], z_ss.at[0], z_rs.at[0], at_z(m), y)

    plane = y_sum(0)
    landed(xr.at[pl.ds(1, NX - 1)], x_rs.at[0])
    for k in range(1, NX):
        plane = plane + xr[k].astype(F32)
    zs[...] = plane.reshape(NZ, 8, 128)
    for m in z_order:
        z_copy(m).start()

    far_backward(2, 1)
    far_backward(3, 1)
    key_out = pltpu.make_async_copy(dko, dk_out.at[0], out_sem.at[1])
    value_out = pltpu.make_async_copy(dvo, dv_out.at[0], out_sem.at[2])
    key_out.start()
    value_out.start()

    def t_copy(dy, dc):
        slot = core * NY + y
        seq = s if dc == 0 else sib
        return send(tiles.at[slot], tiles.at[slot], t_ss.at[0], t_rs.at[0], seq, at_y(dy))

    others = [(dy, dc) for dy in range(NY) for dc in range(2) if (dy, dc) != (0, 0)]

    landed(zr.at[pl.ds(1, NZ - 1)], z_rs.at[0])
    tile = zs[z]
    for m in range(1, NZ):
        tile = tile + zr[m]
    tiles[core * NY + y] = tile
    for dy, dc in others:
        t_copy(dy, dc).start()

    landed(er, e_rs.at[0])
    for h in heads:
        dqo[:, cols(h)] = (dqa[h] + er[h, 0].astype(F32) + er[h, 1].astype(F32)).astype(BF16)
    query_out = pltpu.make_async_copy(dqo, dq_out.at[0], out_sem.at[3])
    query_out.start()

    for ref, sem in (
        (ps, q_ss), (ps, m_ss), (dsend, d_ss), (es, e_ss), (ogs, o_ss), (gtb, g_ss), (ya, ya_ss), (yb, yb_ss),
        (xs.at[pl.ds(1, NX - 1)], x_ss), (zs.at[pl.ds(0, NZ - 1)], z_ss),
    ):
        sent(ref, sem.at[0])
    for out in (gate_out, key_out, value_out, query_out):
        out.wait()

    arrived = tiles.at[pl.ds(0, 2 * NY - 1)]
    landed(arrived, t_rs.at[0])
    lower = jnp.broadcast_to(core, (4, 128)) == 0
    for slot in range(2 * NY):
        full = tiles[slot]
        wg_out[:, slot * 128:(slot + 1) * 128] = jnp.where(lower, full[:4], full[4:])
    sent(arrived, t_ss.at[0])


def finish(*refs):
    sem = refs[-1]
    n = len(refs) // 2
    copies = [pltpu.make_async_copy(refs[i], refs[n + i], sem.at[i]) for i in range(n)]
    for copy in copies:
        copy.start()
    for copy in copies:
        copy.wait()


def finished(arrays):
    anywhere = pl.BlockSpec(memory_space=pl.ANY)
    return pl.pallas_call(
        finish,
        out_shape=tuple(jax.ShapeDtypeStruct(a.shape, a.dtype) for a in arrays),
        in_specs=[pl.BlockSpec(memory_space=pltpu.VMEM)] * len(arrays),
        out_specs=(anywhere,) * len(arrays),
        scratch_shapes=[pltpu.SemaphoreType.DMA((len(arrays),))],
        compiler_params=pltpu.CompilerParams(vmem_limit_bytes=16 * 1024 * 1024),
    )(*arrays)


def local(queries, keys, values, gates, out_weight, out_grad, lengths, pattern):
    block = (HEADS, ROWS, HEAD_DIM)
    block_t = (HEADS, HEAD_DIM, ROWS)
    two = (HEADS, BAND, ROWS, HEAD_DIM)
    three = (HEADS, BAND + 1, ROWS, HEAD_DIM)
    band = (BAND + 1, ROWS, ROWS)
    rows = (ROWS, WIDTH)
    vmem = pltpu.VMEM
    smem = pltpu.SMEM
    scratch = [
        smem(lengths.shape, jnp.int32), smem(pattern.shape, jnp.int32),
        vmem(three, BF16), vmem(rows, BF16), vmem(rows, BF16), vmem(rows, BF16),
        vmem((2,) + rows, BF16), vmem(rows, BF16), vmem((WIDTH, MODEL), BF16),
        vmem(block_t, BF16), vmem(block_t, BF16),
        vmem(band, F32), vmem(band, F32), vmem(block, F32), vmem(block, F32),
        vmem(two, BF16), vmem(two, BF16),
        vmem(three, BF16), vmem(two, BF16), vmem(two, BF16), vmem(two, BF16),
        vmem((HEADS, ROWS, ROWS), BF16), vmem((HEADS, PARTS, ROWS, BAND * PART), BF16),
        vmem(block_t, BF16), vmem((HEADS, PARTS, HEAD_DIM, BAND * PART), BF16),
        vmem((HEADS, ROWS, ROWS), F32), vmem((HEADS, PARTS, BAND * PART, ROWS), F32),
        vmem((NZ, NX, 8, 2 * ROWS), F32), vmem((PARTS, WIDTH, PART), BF16), vmem((PARTS, WIDTH, PART), BF16),
        vmem((NX, NY, NZ * 8, 128), F32),
        vmem((NX, 2, NZ * 4, 128), BF16), vmem((NX, 2, NZ * 4, 128), BF16),
        vmem((NX, 2, NZ * 8, 128), BF16), vmem((NX, 2, NZ * 8, 128), BF16),
        vmem((NX, NZ * 8, 128), BF16), vmem((NX, NZ * 8, 128), BF16),
        vmem((NZ, 8, 128), F32), vmem((NZ, 8, 128), F32), vmem((2 * NY, 8, 128), F32),
        vmem(block, F32), vmem(block_t, F32), vmem(block, F32),
        vmem(rows, BF16), vmem(rows, BF16), vmem(rows, BF16), vmem(rows, BF16),
    ]
    dma = pltpu.SemaphoreType.DMA
    one = dma((1,))
    scratch += [dma((13,)), dma((4,))]
    scratch += [one, dma((HEADS, PARTS)), one, dma((PARTS,)), one, dma((HEADS, PARTS)), one, one]
    scratch += [one, one, one, dma((PARTS,)), one, dma((NX,)), one, dma((NX,))]
    scratch += [one] * 6
    anywhere = pl.BlockSpec(memory_space=pl.ANY)
    grad = jax.ShapeDtypeStruct((1, ROWS, WIDTH), BF16)
    operands = (lengths, pattern, queries, keys, values, gates, out_weight, out_grad)
    results = pl.pallas_call(
        kernel,
        out_shape=(grad, grad, grad, grad, jax.ShapeDtypeStruct((WIDTH // N_SEQ, MODEL), F32)),
        in_specs=[anywhere] * len(operands),
        out_specs=(anywhere,) * 4 + (pl.BlockSpec(memory_space=pltpu.VMEM),),
        scratch_shapes=scratch,
        compiler_params=pltpu.CompilerParams(
            collective_id=0, has_side_effects=True, vmem_limit_bytes=40 * 1024 * 1024
        ),
        cost_estimate=pl.CostEstimate(flops=2 * 10**9, bytes_accessed=5 * 2**20, transcendentals=3 * 4 * ROWS * ROWS),
    )(*[pltpu.with_memory_space_constraint(a, pltpu.HBM) for a in operands])
    return finished(results)


def solution(mesh):
    events = P("dp", "seq", None)
    return jax.shard_map(
        local,
        mesh=mesh,
        in_specs=(events, events, events, events, P(), events, P("dp", None), events),
        out_specs=(events, events, events, events, P("seq", None)),
        check_vma=False,
    )
```
